512 devices in a mesh: dp: 64 (over x_lo, z, core), tensor: 8 (over y, x_hi).
Axes of the slice: x: 4 (x_hi: 2, x_lo: 2; x = x_hi * 2 + x_lo), y: 4, z: 16, core: 2. Of those that a mesh axis runs over, the one named last changes fastest.
Arguments:
- hidden_acts: bfloat16 [512, 128, 14336], P('dp', None, 'tensor'), may hold values from -6 to 6
- out_grads: bfloat16 [512, 128, 4096], P('dp', None, 'tensor'), may hold values from -1.25 to 1.25
- proj_in: bfloat16 [14336, 64], P('tensor'), may hold values from -0.046875 to 0.046875
- proj_out: bfloat16 [4096, 64], P('tensor'), may hold values from -0.09375 to 0.09375
- queries: bfloat16 [1024, 4096], P('dp'), may hold values from -6 to 6
Outputs:
- train_grads: bfloat16 [512, 4096], P(('dp', 'tensor'))
- scores: float32 [512, 1024], P(('dp', 'tensor'))
The draws below stay inside these ranges and needn't reach their ends.
All inputs are finite; a program needn't handle non-finite values.
Results may differ from the reference program's by a relative error of at most 0.0057.
Values may be sent and summed in bfloat16 or wider, within the bound.
A program may use at most 64 MiB of HBM per device.

```python
import jax
import jax.numpy as jnp

D = 4096
FF = 14336
RANK = 64
SEQ = 128
EX = 512
NQ = 1024


def block_levels(own_key, dims, split, smallest, largest):
    loudness = 1.0
    for position, shards_of in split:
        draws = jax.random.uniform(jax.random.fold_in(jax.random.fold_in(own_key, 6), position), (shards_of,), jnp.float32, smallest / len(split), largest / len(split))
        loudness = loudness * jnp.repeat(jnp.exp(draws), dims[position] // shards_of).reshape((-1,) + (1,) * (len(dims) - 1 - position))
    return loudness


def noise(rng, shape, deviation, limit, shards=(), kind=jnp.bfloat16):
    loudness = block_levels(rng, shape, shards, -0.22, 0.18) if shards else 1.0
    array = jax.random.normal(rng, shape, jnp.float32) * deviation * loudness
    return jnp.minimum(jnp.maximum(array, -limit), limit).astype(kind)


def setup_inputs(seed: int = 0) -> dict:
    arg_keys = jax.random.split(jax.random.key(seed), 6)
    hidden_acts = noise(arg_keys[0], (EX, SEQ, FF), 1.0, 6.0, ((0, 64), (2, 8)))
    out_grads = noise(arg_keys[1], (EX, SEQ, D), 0.09, 1.25, ((0, 64), (2, 8)))
    proj_in = noise(arg_keys[2], (FF, RANK), FF ** -0.5, 0.046875, ((0, 8),))
    proj_out = noise(arg_keys[3], (D, RANK), D ** -0.5, 0.09375, ((0, 8),))
    queries = noise(arg_keys[4], (NQ, RANK * RANK), 1.0, 6.0, ((0, 64),))
    return dict(hidden_acts=hidden_acts, out_grads=out_grads, proj_in=proj_in, proj_out=proj_out, queries=queries)


def reference(hidden_acts, out_grads, proj_in, proj_out, queries):
    count = hidden_acts.shape[0]
    act_proj = jnp.dot(hidden_acts.reshape(count * SEQ, FF), proj_in, preferred_element_type=jnp.float32).astype(jnp.bfloat16).reshape(count, SEQ, RANK)
    grad_proj = jnp.dot(out_grads.reshape(count * SEQ, D), proj_out, preferred_element_type=jnp.float32).astype(jnp.bfloat16).reshape(count, SEQ, RANK)
    outer = jnp.einsum("esi,esj->eij", grad_proj.astype(jnp.float32), act_proj.astype(jnp.float32))
    train_grads = outer.reshape(count, RANK * RANK).astype(jnp.bfloat16)
    scores = jnp.einsum("ek,qk->eq", train_grads.astype(jnp.float32), queries.astype(jnp.float32)) / RANK
    return train_grads, scores
```

```python
import functools

import jax
import jax.numpy as jnp
from jax import lax
from jax.experimental import pallas as pl
from jax.experimental.pallas import tpu as pltpu
from jax.sharding import PartitionSpec as P

MESH = pl.DeviceIdType.MESH
SIZES = dict(x_lo=2, z=16, core=2, y=4, x_hi=2)
F32, BF16 = jnp.float32, jnp.bfloat16

TENSOR = [(2, 1), (1, 1), (3, 1), (2, 0), (0, 1), (1, 0), (3, 0), (0, 0)]
PLANE = [(y, h, l, c) for y, h in TENSOR for l in (1, 0) for c in (1, 0)]
OPPOSITE = (2, 1, 0, 0)


def position():
    dp, tensor = lax.axis_index("dp"), lax.axis_index("tensor")
    return dict(
        x_lo=dp // 32, z=lax.rem(dp // 2, 16), core=lax.rem(dp, 2), y=tensor // 2, x_hi=lax.rem(tensor, 2)
    )


def at(place, **offsets):
    moved = {k: lax.rem(v + offsets.get(k, 0) + SIZES[k], SIZES[k]) for k, v in place.items()}
    return {
        "dp": moved["x_lo"] * 32 + moved["z"] * 2 + moved["core"],
        "tensor": moved["y"] * 2 + moved["x_hi"],
    }


def in_plane(place, offset):
    return at(place, **dict(zip(("y", "x_hi", "x_lo", "core"), offset)))


def nt(a, b):
    return lax.dot_general(a, b, (((1,), (1,)), ((), ())), preferred_element_type=F32)


def kernel(
    hidden, grads, w_in, w_out, queries, tg_out, scores_out,
    h_buf, g_buf, win_buf, wout_raw, wout_f32, wout_buf,
    part_send, part_recv, own_part,
    t_send, t_recv, tg_send, tg_recv, q_buf, s_send, s_recv,
    h_sem, g_sem, w_sem,
    part_ssem, part_rsem, t_ssem, t_rsem, tg_ssem, tg_rsem,
    q_ssem, q_rsem, far_ssem, far_rsem, sib_ssem, fwd_ssem, s_ssem, s_rsem,
):
    me = position()
    tensor = lax.axis_index("tensor")

    loads = [
        pltpu.make_async_copy(w_out, wout_raw, w_sem.at[0]),
        pltpu.make_async_copy(w_in, win_buf, w_sem.at[1]),
    ]
    for c in loads:
        c.start()
    reads = []
    for k, (y, h) in enumerate(TENSOR):
        example = lax.rem(me["y"] + y + 2, 4) * 2 + lax.rem(me["x_hi"] + h + 1, 2)
        pair = (
            pltpu.make_async_copy(grads.at[example], g_buf.at[k], g_sem.at[k]),
            pltpu.make_async_copy(hidden.at[example], h_buf.at[k], h_sem.at[k]),
        )
        for c in pair:
            c.start()
        reads.append(pair)

    barrier = pltpu.get_barrier_semaphore()
    for off in PLANE[:-1]:
        pl.semaphore_signal(barrier, inc=1, device_id=in_plane(me, off), device_id_type=MESH)
    for d in (4, -4, 3, -3, 2, -2, 1, -1):
        for c in (0, 1):
            pl.semaphore_signal(barrier, inc=1, device_id=at(me, z=d, core=c), device_id_type=MESH)

    loads[0].wait()
    for j in range(4):
        lanes = slice(128 * j, 128 * j + 128)
        wout_f32[j] = wout_raw[:, lanes].astype(F32)
        wout_buf[0:32, lanes] = wout_f32[j, pl.ds(0, 32, stride=2), :].astype(BF16)
        wout_buf[32:64, lanes] = wout_f32[j, pl.ds(1, 32, stride=2), :].astype(BF16)
    loads[1].wait()

    def partial(k):
        for c in reads[k]:
            c.wait()
        return nt(wout_buf[...], g_buf[k]), nt(win_buf[...], h_buf[k])

    for k in range(7):
        a, b = partial(k)
        part_send[k, 0:64, :] = a.astype(BF16)
        part_send[k, 64:128, :] = b.astype(BF16)
        if k == EARLY - 1:
            pl.semaphore_wait(barrier, 47)
            for j in range(k):
                send_part(j, me, part_send, part_recv, part_ssem, part_rsem).start()
        if k >= EARLY - 1:
            send_part(k, me, part_send, part_recv, part_ssem, part_rsem).start()
        if k == EARLY - 1:
            half = me["z"] // 8
            slot = lax.rem(me["z"], 8) * 2 + me["core"]
            mine = queries.at[:, pl.ds(pl.multiple_of(tensor * 512, 512), 512)]

            def near(d, ssem, rsem):
                target = at(dict(me, core=half), z=d)
                return pltpu.make_async_remote_copy(
                    mine, q_buf.at[slot], ssem, rsem, device_id=target, device_id_type=MESH
                )

            for d in (4, -4):
                near(d, far_ssem, far_rsem).start()
            for d in (3, -3, 2, -2, 1, -1):
                near(d, q_ssem, q_rsem).start()
            sibling = near(0, sib_ssem, q_rsem)
            own = pltpu.make_async_copy(mine, q_buf.at[slot], q_rsem)

            @pl.when(half == me["core"])
            def _():
                own.start()

            @pl.when(half != me["core"])
            def _():
                sibling.start()

    a, b = partial(7)
    own_part[0:64, :] = a
    own_part[64:128, :] = b

    back = lax.rem(me["z"] + 12, 16)
    up = (back // 8) == me["core"]
    sign = jnp.where(up, 1, -1)
    source = lax.rem(me["z"] - 4 * sign + 16, 16)
    first = lax.rem(source, 8) * 2
    pltpu.make_async_copy(q_buf.at[pl.ds(0, 2)], q_buf.at[pl.ds(0, 2)], far_rsem).wait()
    for c, d in ((0, 3), (1, 3), (0, 2), (1, 2), (0, 1), (1, 1), (None, 4)):
        block = first + (jnp.where(up, 0, 1) if c is None else c)
        pltpu.make_async_remote_copy(
            q_buf.at[block], q_buf.at[block], fwd_ssem, q_rsem,
            device_id=at(me, z=sign * d), device_id_type=MESH,
        ).start()

    pltpu.make_async_copy(part_recv, part_recv, part_rsem).wait()
    total = own_part[...]
    for k in range(7):
        total += part_recv[k].astype(F32)
    total = total.astype(BF16)
    act = total[64:128]
    both = nt(total[0:64], jnp.concatenate([act, act], axis=0))
    lane = lax.broadcasted_iota(jnp.int32, (32, 128), 1)
    rows = jnp.where(lane < 64, both[0:32], both[32:64]).astype(BF16)
    tg_send[...] = rows
    wide = rows.astype(F32)
    for k in range(8):
        t_send[k] = wide[4 * k : 4 * k + 4]

    for s, off in enumerate(PLANE[:-1]):
        target = in_plane(me, off)
        pltpu.make_async_remote_copy(
            t_send.at[target["tensor"]], t_recv.at[s], t_ssem, t_rsem, device_id=target, device_id_type=MESH
        ).start()
    pltpu.make_async_copy(t_send.at[tensor], t_recv.at[31], t_rsem).start()
    whole = pltpu.make_async_remote_copy(
        tg_send, tg_recv, tg_ssem, tg_rsem, device_id=in_plane(me, OPPOSITE), device_id_type=MESH
    )
    whole.start()

    pltpu.make_async_copy(q_buf.at[pl.ds(0, 14)], q_buf.at[pl.ds(0, 14)], q_rsem).wait()
    pltpu.make_async_copy(t_recv, t_recv, t_rsem).wait()
    x = jnp.concatenate([t_recv[:, k, :] for k in range(4)], axis=1).astype(BF16)
    part = nt(x, q_buf[...].reshape(256, 512)) * (1.0 / 64)
    for k in range(2):
        s_send[:, k, :] = part[:, 128 * k : 128 * k + 128]
    place = (me["x_lo"] * 2 + me["core"]) * 8 + tensor
    for s, off in enumerate(PLANE):
        if off == OPPOSITE:
            pltpu.make_async_copy(s_send.at[s], s_recv.at[place], s_rsem).start()
            continue
        back = tuple(o - p for o, p in zip(OPPOSITE, off))
        pltpu.make_async_remote_copy(
            s_send.at[s], s_recv.at[place], s_ssem, s_rsem, device_id=in_plane(me, back), device_id_type=MESH
        ).start()

    pltpu.make_async_copy(part_send, part_send, part_ssem).wait()
    pltpu.make_async_copy(t_recv.at[pl.ds(0, 31)], t_recv.at[pl.ds(0, 31)], t_ssem).wait()
    whole.wait_send()
    pltpu.make_async_copy(q_buf.at[pl.ds(0, 2)], q_buf.at[pl.ds(0, 2)], far_ssem).wait()
    pltpu.make_async_copy(q_buf.at[pl.ds(0, 6)], q_buf.at[pl.ds(0, 6)], q_ssem).wait()
    pltpu.make_async_copy(q_buf.at[pl.ds(0, 7)], q_buf.at[pl.ds(0, 7)], fwd_ssem).wait()

    @pl.when(half != me["core"])
    def _():
        sibling.wait_send()

    whole.wait_recv()
    tg_out[...] = tg_recv[...]

    pltpu.make_async_copy(s_recv, s_recv, s_rsem).wait()
    for w in range(4):
        scores_out[2 * w : 2 * w + 2, :] = jnp.sum(s_recv[8 * w : 8 * w + 8], axis=0)
    pltpu.make_async_copy(s_recv.at[pl.ds(0, 31)], s_recv.at[pl.ds(0, 31)], s_ssem).wait()


EARLY = 3


def send_part(k, me, part_send, part_recv, ssem, rsem):
    y, h = TENSOR[k]
    return pltpu.make_async_remote_copy(
        part_send.at[k], part_recv.at[k], ssem, rsem, device_id=at(me, y=y, x_hi=h), device_id_type=MESH
    )


def local(hidden_acts, out_grads, proj_in, proj_out, queries):
    dma = pltpu.SemaphoreType.DMA
    tg, scores = pl.pallas_call(
        kernel,
        name="influence",
        out_shape=(jax.ShapeDtypeStruct((32, 128), BF16), jax.ShapeDtypeStruct((8, 128), F32)),
        in_specs=[pl.BlockSpec(memory_space=pl.ANY)] * 5,
        out_specs=(pl.BlockSpec(memory_space=pltpu.VMEM),) * 2,
        scratch_shapes=[
            pltpu.VMEM((8, 128, 1792), BF16),
            pltpu.VMEM((8, 128, 512), BF16),
            pltpu.VMEM((64, 1792), BF16),
            pltpu.VMEM((64, 512), BF16),
            pltpu.VMEM((4, 64, 128), F32),
            pltpu.VMEM((64, 512), BF16),
            pltpu.VMEM((7, 128, 128), BF16),
            pltpu.VMEM((7, 128, 128), BF16),
            pltpu.VMEM((128, 128), F32),
            pltpu.VMEM((8, 4, 128), F32),
            pltpu.VMEM((32, 4, 128), F32),
            pltpu.VMEM((32, 128), BF16),
            pltpu.VMEM((32, 128), BF16),
            pltpu.VMEM((16, 16, 512), BF16),
            pltpu.VMEM((32, 2, 128), F32),
            pltpu.VMEM((32, 2, 128), F32),
            dma((8,)), dma((8,)), dma((2,)),
        ] + [dma] * 14,
        compiler_params=pltpu.CompilerParams(
            collective_id=0, has_side_effects=True, vmem_limit_bytes=56 * 1024 * 1024
        ),
    )(hidden_acts, out_grads, proj_in.T, proj_out.T, queries)
    return tg.reshape(1, 4096), scores.reshape(1, 1024)


def solution(mesh):
    in_specs = (
        P("dp", None, "tensor"),
        P("dp", None, "tensor"),
        P("tensor", None),
        P("tensor", None),
        P("dp", None),
    )
    out_specs = (P(("dp", "tensor"), None), P(("dp", "tensor"), None))
    return jax.shard_map(local, mesh=mesh, in_specs=in_specs, out_specs=out_specs, check_vma=False)
```

```python
import functools

import jax
import jax.numpy as jnp
from jax import lax
from jax.experimental import pallas as pl
from jax.experimental.pallas import tpu as pltpu
from jax.sharding import PartitionSpec as P

MESH = pl.DeviceIdType.MESH
SIZES = dict(x_lo=2, z=16, core=2, y=4, x_hi=2)
F32, BF16 = jnp.float32, jnp.bfloat16

TENSOR = [(2, 1), (1, 1), (3, 1), (2, 0), (0, 1), (1, 0), (3, 0), (0, 0)]
PLANE = [(y, h, l, c) for y, h in TENSOR for l in (1, 0) for c in (1, 0)]
OPPOSITE = (2, 1, 0, 0)


def position():
    dp, tensor = lax.axis_index("dp"), lax.axis_index("tensor")
    return dict(
        x_lo=dp // 32, z=lax.rem(dp // 2, 16), core=lax.rem(dp, 2), y=tensor // 2, x_hi=lax.rem(tensor, 2)
    )


def at(place, **offsets):
    moved = {k: lax.rem(v + offsets.get(k, 0) + SIZES[k], SIZES[k]) for k, v in place.items()}
    return {
        "dp": moved["x_lo"] * 32 + moved["z"] * 2 + moved["core"],
        "tensor": moved["y"] * 2 + moved["x_hi"],
    }


def in_plane(place, offset):
    return at(place, **dict(zip(("y", "x_hi", "x_lo", "core"), offset)))


def nt(a, b):
    return lax.dot_general(a, b, (((1,), (1,)), ((), ())), preferred_element_type=F32)


def kernel(
    hidden, grads, w_in, w_out, queries, tg_out, scores_out,
    h_buf, g_buf, win_buf, wout_raw, wout_f32, wout_buf,
    part_send, part_recv,
    t_send, t_recv, tg_send, tg_recv, q_buf, s_send, s_recv,
    h_sem, g_sem, w_sem,
    part_ssem, part_rsem, t_ssem, t_rsem, tg_ssem, tg_rsem,
    q_ssem, q_rsem, far_ssem, far_rsem, sib_ssem, fwd_ssem, s_ssem, s_rsem,
):
    me = position()
    tensor = lax.axis_index("tensor")

    loads = [
        pltpu.make_async_copy(w_out, wout_raw, w_sem.at[0]),
        pltpu.make_async_copy(w_in, win_buf, w_sem.at[1]),
    ]
    for c in loads:
        c.start()
    reads = []
    for k in range(2):
        four = pl.ds(4 * k, 4)
        pair = (
            pltpu.make_async_copy(grads.at[four], g_buf.at[four], g_sem.at[k]),
            pltpu.make_async_copy(hidden.at[four], h_buf.at[four], h_sem.at[k]),
        )
        for c in pair:
            c.start()
        reads.append(pair)

    barrier = pltpu.get_barrier_semaphore()
    for off in PLANE[:-1]:
        pl.semaphore_signal(barrier, inc=1, device_id=in_plane(me, off), device_id_type=MESH)
    for d in (4, -4, 3, -3, 2, -2, 1, -1):
        for c in (0, 1):
            pl.semaphore_signal(barrier, inc=1, device_id=at(me, z=d, core=c), device_id_type=MESH)

    loads[0].wait()
    for j in range(4):
        lanes = slice(128 * j, 128 * j + 128)
        wout_f32[j] = wout_raw[:, lanes].astype(F32)
        wout_buf[0:32, lanes] = wout_f32[j, pl.ds(0, 32, stride=2), :].astype(BF16)
        wout_buf[32:64, lanes] = wout_f32[j, pl.ds(1, 32, stride=2), :].astype(BF16)
    loads[1].wait()

    for k in range(2):
        for c in reads[k]:
            c.wait()
        four = pl.ds(4 * k, 4)
        a = nt(wout_buf[...], g_buf[four].reshape(512, 512)).astype(BF16)
        b = nt(win_buf[...], h_buf[four].reshape(512, 1792)).astype(BF16)
        for j in range(4):
            part_send[4 * k + j, 0:64, :] = a[:, 128 * j : 128 * j + 128]
            part_send[4 * k + j, 64:128, :] = b[:, 128 * j : 128 * j + 128]

    pl.semaphore_wait(barrier, 47)
    for k, (y, h) in enumerate(TENSOR):
        example = lax.rem(me["y"] + y + 2, 4) * 2 + lax.rem(me["x_hi"] + h + 1, 2)
        if k == 7:
            pltpu.make_async_copy(part_send.at[example], part_recv.at[k], part_rsem).start()
            continue
        pltpu.make_async_remote_copy(
            part_send.at[example], part_recv.at[k], part_ssem, part_rsem,
            device_id=at(me, y=y, x_hi=h), device_id_type=MESH,
        ).start()

    half = me["z"] // 8
    slot = lax.rem(me["z"], 8) * 2 + me["core"]
    mine = queries.at[:, pl.ds(pl.multiple_of(tensor * 512, 512), 512)]

    def near(d, ssem, rsem):
        target = at(dict(me, core=half), z=d)
        return pltpu.make_async_remote_copy(
            mine, q_buf.at[slot], ssem, rsem, device_id=target, device_id_type=MESH
        )

    for d in (4, -4):
        near(d, far_ssem, far_rsem).start()
    for d in (3, -3, 2, -2, 1, -1):
        near(d, q_ssem, q_rsem).start()
    sibling = near(0, sib_ssem, q_rsem)
    own = pltpu.make_async_copy(mine, q_buf.at[slot], q_rsem)

    @pl.when(half == me["core"])
    def _():
        own.start()

    @pl.when(half != me["core"])
    def _():
        sibling.start()

    back = lax.rem(me["z"] + 12, 16)
    up = (back // 8) == me["core"]
    sign = jnp.where(up, 1, -1)
    source = lax.rem(me["z"] - 4 * sign + 16, 16)
    first = lax.rem(source, 8) * 2
    pltpu.make_async_copy(q_buf.at[pl.ds(0, 2)], q_buf.at[pl.ds(0, 2)], far_rsem).wait()
    for c, d in ((0, 3), (1, 3), (0, 2), (1, 2), (0, 1), (1, 1), (None, 4)):
        block = first + (jnp.where(up, 0, 1) if c is None else c)
        pltpu.make_async_remote_copy(
            q_buf.at[block], q_buf.at[block], fwd_ssem, q_rsem,
            device_id=at(me, z=sign * d), device_id_type=MESH,
        ).start()

    pltpu.make_async_copy(part_recv, part_recv, part_rsem).wait()
    total = part_recv[0].astype(F32)
    for k in range(1, 8):
        total += part_recv[k].astype(F32)
    total = total.astype(BF16)
    act = total[64:128]
    both = nt(total[0:64], jnp.concatenate([act, act], axis=0))
    lane = lax.broadcasted_iota(jnp.int32, (32, 128), 1)
    rows = jnp.where(lane < 64, both[0:32], both[32:64]).astype(BF16)
    tg_send[...] = rows
    wide = rows.astype(F32)
    for k in range(8):
        t_send[k] = wide[4 * k : 4 * k + 4]

    for s, off in enumerate(PLANE[:-1]):
        target = in_plane(me, off)
        pltpu.make_async_remote_copy(
            t_send.at[target["tensor"]], t_recv.at[s], t_ssem, t_rsem, device_id=target, device_id_type=MESH
        ).start()
    pltpu.make_async_copy(t_send.at[tensor], t_recv.at[31], t_rsem).start()
    whole = pltpu.make_async_remote_copy(
        tg_send, tg_recv, tg_ssem, tg_rsem, device_id=in_plane(me, OPPOSITE), device_id_type=MESH
    )
    whole.start()

    pltpu.make_async_copy(q_buf.at[pl.ds(0, 14)], q_buf.at[pl.ds(0, 14)], q_rsem).wait()
    pltpu.make_async_copy(t_recv, t_recv, t_rsem).wait()
    x = jnp.concatenate([t_recv[:, k, :] for k in range(4)], axis=1).astype(BF16)
    part = nt(x, q_buf[...].reshape(256, 512)) * (1.0 / 64)
    for k in range(2):
        s_send[:, k, :] = part[:, 128 * k : 128 * k + 128]
    place = (me["x_lo"] * 2 + me["core"]) * 8 + tensor
    for s, off in enumerate(PLANE):
        if off == OPPOSITE:
            pltpu.make_async_copy(s_send.at[s], s_recv.at[place], s_rsem).start()
            continue
        back = tuple(o - p for o, p in zip(OPPOSITE, off))
        pltpu.make_async_remote_copy(
            s_send.at[s], s_recv.at[place], s_ssem, s_rsem, device_id=in_plane(me, back), device_id_type=MESH
        ).start()

    pltpu.make_async_copy(part_send.at[pl.ds(0, 7)], part_send.at[pl.ds(0, 7)], part_ssem).wait()
    pltpu.make_async_copy(t_recv.at[pl.ds(0, 31)], t_recv.at[pl.ds(0, 31)], t_ssem).wait()
    whole.wait_send()
    pltpu.make_async_copy(q_buf.at[pl.ds(0, 2)], q_buf.at[pl.ds(0, 2)], far_ssem).wait()
    pltpu.make_async_copy(q_buf.at[pl.ds(0, 6)], q_buf.at[pl.ds(0, 6)], q_ssem).wait()
    pltpu.make_async_copy(q_buf.at[pl.ds(0, 7)], q_buf.at[pl.ds(0, 7)], fwd_ssem).wait()

    @pl.when(half != me["core"])
    def _():
        sibling.wait_send()

    whole.wait_recv()
    tg_out[...] = tg_recv[...]

    pltpu.make_async_copy(s_recv, s_recv, s_rsem).wait()
    for w in range(4):
        scores_out[2 * w : 2 * w + 2, :] = jnp.sum(s_recv[8 * w : 8 * w + 8], axis=0)
    pltpu.make_async_copy(s_recv.at[pl.ds(0, 31)], s_recv.at[pl.ds(0, 31)], s_ssem).wait()


def finish(tg, part, tg_out, scores_out):
    tg_out[...] = tg[...].reshape(1, 4096)
    scores_out[...] = part[...].reshape(1, 1024)


def local(hidden_acts, out_grads, proj_in, proj_out, queries):
    dma = pltpu.SemaphoreType.DMA
    tg, scores = pl.pallas_call(
        kernel,
        name="influence",
        out_shape=(jax.ShapeDtypeStruct((32, 128), BF16), jax.ShapeDtypeStruct((8, 128), F32)),
        in_specs=[pl.BlockSpec(memory_space=pl.ANY)] * 5,
        out_specs=(pl.BlockSpec(memory_space=pltpu.VMEM),) * 2,
        scratch_shapes=[
            pltpu.VMEM((8, 128, 1792), BF16),
            pltpu.VMEM((8, 128, 512), BF16),
            pltpu.VMEM((64, 1792), BF16),
            pltpu.VMEM((64, 512), BF16),
            pltpu.VMEM((4, 64, 128), F32),
            pltpu.VMEM((64, 512), BF16),
            pltpu.VMEM((8, 128, 128), BF16),
            pltpu.VMEM((8, 128, 128), BF16),
            pltpu.VMEM((8, 4, 128), F32),
            pltpu.VMEM((32, 4, 128), F32),
            pltpu.VMEM((32, 128), BF16),
            pltpu.VMEM((32, 128), BF16),
            pltpu.VMEM((16, 16, 512), BF16),
            pltpu.VMEM((32, 2, 128), F32),
            pltpu.VMEM((32, 2, 128), F32),
            dma((2,)), dma((2,)), dma((2,)),
        ] + [dma] * 14,
        compiler_params=pltpu.CompilerParams(
            collective_id=0, has_side_effects=True, vmem_limit_bytes=56 * 1024 * 1024
        ),
    )(hidden_acts, out_grads, proj_in.T, proj_out.T, queries)
    return pl.pallas_call(
        finish,
        name="finish",
        out_shape=(jax.ShapeDtypeStruct((1, 4096), BF16), jax.ShapeDtypeStruct((1, 1024), F32)),
    )(tg, scores)


def solution(mesh):
    in_specs = (
        P("dp", None, "tensor"),
        P("dp", None, "tensor"),
        P("tensor", None),
        P("tensor", None),
        P("dp", None),
    )
    out_specs = (P(("dp", "tensor"), None), P(("dp", "tensor"), None))
    return jax.shard_map(local, mesh=mesh, in_specs=in_specs, out_specs=out_specs, check_vma=False)
```

```python
import functools

import jax
import jax.numpy as jnp
from jax import lax
from jax.experimental import pallas as pl
from jax.experimental.pallas import tpu as pltpu
from jax.sharding import PartitionSpec as P

MESH = pl.DeviceIdType.MESH
SIZES = dict(x_lo=2, z=16, core=2, y=4, x_hi=2)
F32, BF16 = jnp.float32, jnp.bfloat16

TENSOR = [(2, 1), (1, 1), (3, 1), (2, 0), (0, 1), (1, 0), (3, 0), (0, 0)]
PLANE = [(y, h, l, c) for y, h in TENSOR for l in (1, 0) for c in (1, 0)]
OPPOSITE = (2, 1, 0, 0)


def position():
    dp, tensor = lax.axis_index("dp"), lax.axis_index("tensor")
    return dict(
        x_lo=dp // 32, z=lax.rem(dp // 2, 16), core=lax.rem(dp, 2), y=tensor // 2, x_hi=lax.rem(tensor, 2)
    )


def at(place, **offsets):
    moved = {k: lax.rem(v + offsets.get(k, 0) + SIZES[k], SIZES[k]) for k, v in place.items()}
    return {
        "dp": moved["x_lo"] * 32 + moved["z"] * 2 + moved["core"],
        "tensor": moved["y"] * 2 + moved["x_hi"],
    }


def in_plane(place, offset):
    return at(place, **dict(zip(("y", "x_hi", "x_lo", "core"), offset)))


def nt(a, b):
    return lax.dot_general(a, b, (((1,), (1,)), ((), ())), preferred_element_type=F32)


def arrived(buffer, semaphore):
    pltpu.make_async_copy(buffer, buffer, semaphore).wait()


def kernel(
    hidden, grads, w_in, w_out, queries, tg_out, scores_out,
    h_buf, g_buf, win_buf, wout_raw, wout_f32, wout_buf,
    part_send, part_recv,
    t_send, t_recv, tg_send, tg_recv, q_buf, s_send, s_recv,
    h_sem, g_sem, w_sem,
    part_ssem, part_rsem, t_ssem, t_rsem, tg_ssem, tg_rsem,
    q_ssem, q_rsem, far_ssem, far_rsem, sib_ssem, fwd_ssem, s_ssem, s_rsem, direct_ssem, late_ready,
):
    me = position()
    tensor, z, core = lax.axis_index("tensor"), me["z"], me["core"]

    loads = [
        pltpu.make_async_copy(w_out, wout_raw, w_sem.at[0]),
        pltpu.make_async_copy(w_in, win_buf, w_sem.at[1]),
    ]
    for c in loads:
        c.start()
    reads = []
    for k in range(2):
        four = pl.ds(4 * k, 4)
        pair = (
            pltpu.make_async_copy(grads.at[four], g_buf.at[four], g_sem.at[k]),
            pltpu.make_async_copy(hidden.at[four], h_buf.at[four], h_sem.at[k]),
        )
        for c in pair:
            c.start()
        reads.append(pair)

    late = z >= 8
    barrier = pltpu.get_barrier_semaphore()

    def say(semaphore, device):
        pl.semaphore_signal(semaphore, inc=1, device_id=device, device_id_type=MESH)

    def when(condition, action):
        pl.when(condition)(action)

    def to_line(semaphore, d):
        for c in (0, 1):
            say(semaphore, at(dict(me, core=c), z=d))

    for far in range(8, 16):
        window = jnp.logical_or(far - z <= 4, far - z >= 12)
        when(jnp.logical_and(jnp.logical_not(late), jnp.logical_or(core == 1, window)), functools.partial(to_line, barrier, far - z))
    for off in PLANE[:-1]:
        say(barrier, in_plane(me, off))
    for d in (7, 6, 5):
        when(z + d < 8, functools.partial(to_line, barrier, d))
    for d in (4, -4, 3, -3, 2, -2, 1, -1):
        when((z + d) // 8 == z // 8, functools.partial(to_line, barrier, d))
    place = lax.rem(z, 8)
    same = jnp.minimum(place, 4) + jnp.minimum(7 - place, 4)
    close = jnp.where(z < 12, 12 - z, z - 11)
    expected = 31 + 2 * same + jnp.where(late, close + 8, 2 * jnp.maximum(z - 4, 0))

    loads[0].wait()
    for j in range(4):
        lanes = slice(128 * j, 128 * j + 128)
        wout_f32[j] = wout_raw[:, lanes].astype(F32)
        wout_buf[0:32, lanes] = wout_f32[j, pl.ds(0, 32, stride=2), :].astype(BF16)
        wout_buf[32:64, lanes] = wout_f32[j, pl.ds(1, 32, stride=2), :].astype(BF16)
    loads[1].wait()

    for k in range(2):
        for c in reads[k]:
            c.wait()
        four = pl.ds(4 * k, 4)
        a = nt(wout_buf[...], g_buf[four].reshape(512, 512)).astype(BF16)
        b = nt(win_buf[...], h_buf[four].reshape(512, 1792)).astype(BF16)
        for j in range(4):
            part_send[4 * k + j, 0:64, :] = a[:, 128 * j : 128 * j + 128]
            part_send[4 * k + j, 64:128, :] = b[:, 128 * j : 128 * j + 128]

    pl.semaphore_wait(barrier, expected)

    half = z // 8
    slot = place * 2 + core
    mine = queries.at[:, pl.ds(pl.multiple_of(tensor * 512, 512), 512)]

    def near(d, ssem=q_ssem, rsem=q_rsem):
        if isinstance(d, int) and abs(d) == 4:
            ssem, rsem = far_ssem, far_rsem
        return pltpu.make_async_remote_copy(
            mine, q_buf.at[slot], ssem, rsem, device_id=at(dict(me, core=half), z=d), device_id_type=MESH
        )

    relay = lax.rem(z + 4, 8)
    when(late, lambda: near(16 + relay - z, far_ssem, far_rsem).start())
    high, low = jnp.logical_and(late, z >= 12), jnp.logical_and(late, z < 12)
    directs = []
    for k in range(8):
        goes = jnp.logical_and(relay != k, late if k < 2 else high if k < 4 else low)
        directs.append((goes, near(16 + k - z, direct_ssem)))
        when(goes, lambda k=k: directs[k][1].start())

    for k, (y, h) in enumerate(TENSOR):
        example = lax.rem(me["y"] + y + 2, 4) * 2 + lax.rem(me["x_hi"] + h + 1, 2)
        if k == 7:
            pltpu.make_async_copy(part_send.at[example], part_recv.at[k], part_rsem).start()
            continue
        pltpu.make_async_remote_copy(
            part_send.at[example], part_recv.at[k], part_ssem, part_rsem,
            device_id=at(me, y=y, x_hi=h), device_id_type=MESH,
        ).start()

    for d in (-4, 4, -3, 3, -2, 2, -1, 1):
        when((z + d) // 8 == half, lambda d=d: near(d).start())
    sibling = near(0, sib_ssem)
    own = pltpu.make_async_copy(mine, q_buf.at[slot], q_rsem)
    when(half == core, lambda: own.start())
    when(half != core, lambda: sibling.start())
    for d in (4, 3, 2, 1):
        when(jnp.logical_and(late, jnp.logical_and(z - d < 8, z - d >= 4)), functools.partial(to_line, late_ready, -d))
        when(z + d >= 16, functools.partial(to_line, late_ready, d))
    for d in (7, 6, 5):
        when(jnp.logical_and(z < 8, z - d >= 0), functools.partial(to_line, late_ready, -d))

    arrived(part_recv, part_rsem)
    total = part_recv[0].astype(F32)
    for k in range(1, 8):
        total += part_recv[k].astype(F32)
    total = total.astype(BF16)
    act = total[64:128]
    both = nt(total[0:64], jnp.concatenate([act, act], axis=0))
    lane = lax.broadcasted_iota(jnp.int32, (32, 128), 1)
    rows = jnp.where(lane < 64, both[0:32], both[32:64]).astype(BF16)
    tg_send[...] = rows
    wide = rows.astype(F32)
    for k in range(8):
        t_send[k] = wide[4 * k : 4 * k + 4]

    for s, off in enumerate(PLANE[:-1]):
        target = in_plane(me, off)
        pltpu.make_async_remote_copy(
            t_send.at[target["tensor"]], t_recv.at[s], t_ssem, t_rsem, device_id=target, device_id_type=MESH
        ).start()
    pltpu.make_async_copy(t_send.at[tensor], t_recv.at[31], t_rsem).start()
    whole = pltpu.make_async_remote_copy(
        tg_send, tg_recv, tg_ssem, tg_rsem, device_id=in_plane(me, OPPOSITE), device_id_type=MESH
    )
    whole.start()

    answers = jnp.where(z < 4, 4 - z, z - 3) + jnp.maximum(3 - z, 0)
    when(jnp.logical_not(late), lambda: pl.semaphore_wait(late_ready, 2 * answers))
    for d in (4, 3, 2, 1):
        when(z - d < 0, lambda d=d: near(-d).start())
        when(jnp.logical_and(jnp.logical_not(late), z + d >= 8), lambda d=d: near(d).start())

    up = (lax.rem(z + 12, 16) // 8) == core
    sign = jnp.where(up, 1, -1)
    first = lax.rem(lax.rem(z - 4 * sign + 16, 16), 8) * 2
    arrived(q_buf.at[pl.ds(0, 2)], far_rsem)
    wanted = []
    for c, d in ((None, 4), (0, 3), (1, 3), (0, 2), (1, 2), (0, 1), (1, 1)):
        block = first + (jnp.where(up, 0, 1) if c is None else c)
        goal = lax.rem(z + sign * d + 16, 16)
        copy = pltpu.make_async_remote_copy(
            q_buf.at[block], q_buf.at[block], fwd_ssem, q_rsem,
            device_id=at(me, z=sign * d), device_id_type=MESH,
        )
        wanted.append((jnp.logical_or(core == 0, goal >= 8), copy))
        when(wanted[-1][0], lambda copy=copy: copy.start())
    holds = jnp.logical_and(core == 1, jnp.logical_not(late))
    for goal in (2, 3, 4, 5, 6, 7):
        for c in (0, 1):
            copy = pltpu.make_async_remote_copy(
                q_buf.at[first + c], q_buf.at[first + c], fwd_ssem, q_rsem,
                device_id=at(me, z=goal - z + 16), device_id_type=MESH,
            )
            wanted.append((jnp.logical_and(holds, z >= 4 if goal < 4 else z < 4), copy))
            when(wanted[-1][0], lambda copy=copy: copy.start())

    arrived(q_buf.at[pl.ds(0, 14)], q_rsem)
    arrived(t_recv, t_rsem)
    x = jnp.concatenate([t_recv[:, k, :] for k in range(4)], axis=1).astype(BF16)
    part = nt(x, q_buf[...].reshape(256, 512)) * (1.0 / 64)
    for k in range(2):
        s_send[:, k, :] = part[:, 128 * k : 128 * k + 128]
    place = (me["x_lo"] * 2 + core) * 8 + tensor
    for s, off in reversed(list(enumerate(PLANE))):
        if off == OPPOSITE:
            pltpu.make_async_copy(s_send.at[s], s_recv.at[place], s_rsem).start()
            continue
        back = tuple(o - p for o, p in zip(OPPOSITE, off))
        pltpu.make_async_remote_copy(
            s_send.at[s], s_recv.at[place], s_ssem, s_rsem, device_id=in_plane(me, back), device_id_type=MESH
        ).start()

    arrived(part_send.at[pl.ds(0, 7)], part_ssem)
    arrived(t_recv.at[pl.ds(0, 31)], t_ssem)
    whole.wait_send()
    arrived(q_buf.at[pl.ds(0, 2)], far_ssem)
    for goes, copy in directs:
        when(goes, lambda copy=copy: copy.wait_send())
    for d in (3, -3, 2, -2, 1, -1):
        when(jnp.logical_or(jnp.logical_not(late), (z + d) // 8 == half), lambda d=d: near(d).wait_send())
    for condition, copy in wanted:
        when(condition, lambda copy=copy: copy.wait_send())
    when(half != core, lambda: sibling.wait_send())

    whole.wait_recv()
    tg_out[...] = tg_recv[...]

    arrived(s_recv, s_rsem)
    for w in range(4):
        scores_out[2 * w : 2 * w + 2, :] = jnp.sum(s_recv[8 * w : 8 * w + 8], axis=0)
    arrived(s_recv.at[pl.ds(0, 31)], s_ssem)


def finish(tg, part, tg_out, scores_out):
    tg_out[...] = tg[...].reshape(1, 4096)
    scores_out[...] = part[...].reshape(1, 1024)


def local(hidden_acts, out_grads, proj_in, proj_out, queries):
    dma = pltpu.SemaphoreType.DMA
    tg, scores = pl.pallas_call(
        kernel,
        name="influence",
        out_shape=(jax.ShapeDtypeStruct((32, 128), BF16), jax.ShapeDtypeStruct((8, 128), F32)),
        in_specs=[pl.BlockSpec(memory_space=pl.ANY)] * 5,
        out_specs=(pl.BlockSpec(memory_space=pltpu.VMEM),) * 2,
        scratch_shapes=[
            pltpu.VMEM((8, 128, 1792), BF16),
            pltpu.VMEM((8, 128, 512), BF16),
            pltpu.VMEM((64, 1792), BF16),
            pltpu.VMEM((64, 512), BF16),
            pltpu.VMEM((4, 64, 128), F32),
            pltpu.VMEM((64, 512), BF16),
            pltpu.VMEM((8, 128, 128), BF16),
            pltpu.VMEM((8, 128, 128), BF16),
            pltpu.VMEM((8, 4, 128), F32),
            pltpu.VMEM((32, 4, 128), F32),
            pltpu.VMEM((32, 128), BF16),
            pltpu.VMEM((32, 128), BF16),
            pltpu.VMEM((16, 16, 512), BF16),
            pltpu.VMEM((32, 2, 128), F32),
            pltpu.VMEM((32, 2, 128), F32),
            dma((2,)), dma((2,)), dma((2,)),
        ] + [dma] * 15 + [pltpu.SemaphoreType.REGULAR],
        compiler_params=pltpu.CompilerParams(
            collective_id=0, has_side_effects=True, vmem_limit_bytes=56 * 1024 * 1024
        ),
    )(hidden_acts, out_grads, proj_in.T, proj_out.T, queries)
    return pl.pallas_call(
        finish,
        name="finish",
        out_shape=(jax.ShapeDtypeStruct((1, 4096), BF16), jax.ShapeDtypeStruct((1, 1024), F32)),
    )(tg, scores)


def solution(mesh):
    in_specs = (
        P("dp", None, "tensor"),
        P("dp", None, "tensor"),
        P("tensor", None),
        P("tensor", None),
        P("dp", None),
    )
    out_specs = (P(("dp", "tensor"), None), P(("dp", "tensor"), None))
    return jax.shard_map(local, mesh=mesh, in_specs=in_specs, out_specs=out_specs, check_vma=False)
```

```python
import functools

import jax
import jax.numpy as jnp
from jax import lax
from jax.experimental import pallas as pl
from jax.experimental.pallas import tpu as pltpu
from jax.sharding import PartitionSpec as P

MESH = pl.DeviceIdType.MESH
SIZES = dict(x_lo=2, z=16, core=2, y=4, x_hi=2)
F32, BF16 = jnp.float32, jnp.bfloat16


def hops(offset):
    y, x_hi, x_lo, _ = offset
    return min(y, 4 - y) + (1 if x_lo else 2 * x_hi)


PLANE = sorted(
    ((y, h, l, c) for y in range(4) for h in range(2) for l in range(2) for c in range(2)),
    key=lambda o: (-hops(o), o == (0, 0, 0, 0), o),
)
TENSOR = [o for o in PLANE if o[2:] == (0, 0)]
OPPOSITE = (2, 1, 0, 0)


def position():
    dp, tensor = lax.axis_index("dp"), lax.axis_index("tensor")
    return dict(
        x_lo=dp // 32, z=lax.rem(dp // 2, 16), core=lax.rem(dp, 2), y=tensor // 2, x_hi=lax.rem(tensor, 2)
    )


def at(place, **offsets):
    moved = {k: lax.rem(v + offsets.get(k, 0) + SIZES[k], SIZES[k]) for k, v in place.items()}
    return {
        "dp": moved["x_lo"] * 32 + moved["z"] * 2 + moved["core"],
        "tensor": moved["y"] * 2 + moved["x_hi"],
    }


def plane_map(place):
    dp = {(l, c): at(place, x_lo=l, core=c)["dp"] for l in range(2) for c in range(2)}
    tensor = {(y, h): at(place, y=y, x_hi=h)["tensor"] for y in range(4) for h in range(2)}
    return {o: {"dp": dp[o[2:]], "tensor": tensor[o[:2]]} for o in PLANE}


def difference(a, b):
    return tuple((p - q) % n for p, q, n in zip(a, b, (4, 2, 2, 2)))


def nt(a, b):
    return lax.dot_general(a, b, (((1,), (1,)), ((), ())), preferred_element_type=F32)


def arrived(buffer, semaphore):
    pltpu.make_async_copy(buffer, buffer, semaphore).wait()


def kernel(
    hidden, grads, w_in, w_out, queries, tg_out, scores_out,
    h_buf, g_buf, win_buf, wout_raw, wout_f32, wout_buf,
    part_send, part_recv,
    t_send, t_recv, tg_send, tg_recv, q_buf, mine, x_buf, s_send, s_recv,
    h_sem, g_sem, w_sem,
    part_ssem, part_rsem, t_ssem, t_rsem, tg_ssem, tg_rsem,
    q_ssem, q_rsem, far_ssem, far_rsem, sib_ssem, fwd_ssem, s_ssem, s_rsem, direct_ssem, late_ready,
):
    me = position()
    tensor, z, core = lax.axis_index("tensor"), me["z"], me["core"]
    device = plane_map(me)

    loads = [
        pltpu.make_async_copy(w_out, wout_raw, w_sem.at[0]),
        pltpu.make_async_copy(w_in, win_buf, w_sem.at[1]),
        pltpu.make_async_copy(
            queries.at[:, pl.ds(pl.multiple_of(tensor * 512, 512), 512)], mine, w_sem.at[2]
        ),
    ]
    for c in loads:
        c.start()
    reads = []
    for k in range(2):
        four = pl.ds(4 * k, 4)
        pair = (
            pltpu.make_async_copy(grads.at[four], g_buf.at[four], g_sem.at[k]),
            pltpu.make_async_copy(hidden.at[four], h_buf.at[four], h_sem.at[k]),
        )
        for c in pair:
            c.start()
        reads.append(pair)

    late = z >= 8
    barrier = pltpu.get_barrier_semaphore()

    def say(semaphore, device):
        pl.semaphore_signal(semaphore, inc=1, device_id=device, device_id_type=MESH)

    def when(condition, action):
        pl.when(condition)(action)

    def to_line(semaphore, d):
        for c in (0, 1):
            say(semaphore, at(dict(me, core=c), z=d))

    for far in range(8, 16):
        window = jnp.logical_or(far - z <= 4, far - z >= 12)
        when(jnp.logical_and(jnp.logical_not(late), jnp.logical_or(core == 1, window)), functools.partial(to_line, barrier, far - z))
    for off in PLANE[:-1]:
        say(barrier, device[off])
    for d in (7, 6, 5):
        when(z + d < 8, functools.partial(to_line, barrier, d))
    for d in (4, -4, 3, -3, 2, -2, 1, -1):
        when((z + d) // 8 == z // 8, functools.partial(to_line, barrier, d))
    place = lax.rem(z, 8)
    same = jnp.minimum(place, 4) + jnp.minimum(7 - place, 4)
    close = jnp.where(z < 12, 12 - z, z - 11)
    expected = 31 + 2 * same + jnp.where(late, close + 8, 2 * jnp.maximum(z - 4, 0))

    loads[0].wait()
    for j in range(4):
        lanes = slice(128 * j, 128 * j + 128)
        wout_f32[j] = wout_raw[:, lanes].astype(F32)
        wout_buf[0:32, lanes] = wout_f32[j, pl.ds(0, 32, stride=2), :].astype(BF16)
        wout_buf[32:64, lanes] = wout_f32[j, pl.ds(1, 32, stride=2), :].astype(BF16)
    loads[1].wait()

    for k in range(2):
        for c in reads[k]:
            c.wait()
        four = pl.ds(4 * k, 4)
        a = nt(wout_buf[...], g_buf[four].reshape(512, 512)).astype(BF16)
        b = nt(win_buf[...], h_buf[four].reshape(512, 1792)).astype(BF16)
        for j in range(4):
            part_send[4 * k + j, 0:64, :] = a[:, 128 * j : 128 * j + 128]
            part_send[4 * k + j, 64:128, :] = b[:, 128 * j : 128 * j + 128]

    pl.semaphore_wait(barrier, expected)

    half = z // 8
    slot = place * 2 + core
    loads[2].wait()

    def near(d, ssem=q_ssem, rsem=q_rsem):
        if isinstance(d, int) and abs(d) == 4:
            ssem, rsem = far_ssem, far_rsem
        return pltpu.make_async_remote_copy(
            mine, q_buf.at[slot], ssem, rsem, device_id=at(dict(me, core=half), z=d), device_id_type=MESH
        )

    relay = lax.rem(z + 4, 8)
    when(late, lambda: near(16 + relay - z, far_ssem, far_rsem).start())
    high, low = jnp.logical_and(late, z >= 12), jnp.logical_and(late, z < 12)
    directs = []
    for k in range(8):
        goes = jnp.logical_and(relay != k, late if k < 2 else high if k < 4 else low)
        directs.append((goes, near(16 + k - z, direct_ssem)))
        when(goes, lambda k=k: directs[k][1].start())

    for k, off in enumerate(TENSOR):
        example = device[difference(off, OPPOSITE)]["tensor"]
        if k == 7:
            pltpu.make_async_copy(part_send.at[example], part_recv.at[k], part_rsem).start()
            continue
        pltpu.make_async_remote_copy(
            part_send.at[example], part_recv.at[k], part_ssem, part_rsem,
            device_id=device[off], device_id_type=MESH,
        ).start()

    for d in (-4, 4, -3, 3, -2, 2, -1, 1):
        when((z + d) // 8 == half, lambda d=d: near(d).start())
    sibling = near(0, sib_ssem)
    own = pltpu.make_async_copy(mine, q_buf.at[slot], q_rsem)
    when(half == core, lambda: own.start())
    when(half != core, lambda: sibling.start())
    for d in (4, 3, 2, 1):
        when(jnp.logical_and(late, jnp.logical_and(z - d < 8, z - d >= 4)), functools.partial(to_line, late_ready, -d))
        when(z + d >= 16, functools.partial(to_line, late_ready, d))
    for d in (7, 6, 5):
        when(jnp.logical_and(z < 8, z - d >= 0), functools.partial(to_line, late_ready, -d))

    arrived(part_recv, part_rsem)
    total = part_recv[0].astype(F32)
    for k in range(1, 8):
        total += part_recv[k].astype(F32)
    total = total.astype(BF16)
    act = total[64:128]
    both = nt(total[0:64], jnp.concatenate([act, act], axis=0))
    lane = lax.broadcasted_iota(jnp.int32, (32, 128), 1)
    rows = jnp.where(lane < 64, both[0:32], both[32:64]).astype(BF16)
    tg_send[...] = rows
    wide = rows.astype(F32)
    for k in range(8):
        t_send[k] = wide[4 * k : 4 * k + 4]

    for s, off in enumerate(PLANE[:-1]):
        target = device[off]
        pltpu.make_async_remote_copy(
            t_send.at[target["tensor"]], t_recv.at[s], t_ssem, t_rsem, device_id=target, device_id_type=MESH
        ).start()
    pltpu.make_async_copy(t_send.at[tensor], t_recv.at[31], t_rsem).start()
    whole = pltpu.make_async_remote_copy(
        tg_send, tg_recv, tg_ssem, tg_rsem, device_id=device[OPPOSITE], device_id_type=MESH
    )
    whole.start()

    answers = jnp.where(z < 4, 4 - z, z - 3) + jnp.maximum(3 - z, 0)
    when(jnp.logical_not(late), lambda: pl.semaphore_wait(late_ready, 2 * answers))
    for d in (4, 3, 2, 1):
        when(z - d < 0, lambda d=d: near(-d).start())
        when(jnp.logical_and(jnp.logical_not(late), z + d >= 8), lambda d=d: near(d).start())

    up = (lax.rem(z + 12, 16) // 8) == core
    sign = jnp.where(up, 1, -1)
    first = lax.rem(lax.rem(z - 4 * sign + 16, 16), 8) * 2
    arrived(q_buf.at[pl.ds(0, 2)], far_rsem)
    wanted = []
    for c, d in ((None, 4), (0, 3), (1, 3), (0, 2), (1, 2), (0, 1), (1, 1)):
        block = first + (jnp.where(up, 0, 1) if c is None else c)
        goal = lax.rem(z + sign * d + 16, 16)
        copy = pltpu.make_async_remote_copy(
            q_buf.at[block], q_buf.at[block], fwd_ssem, q_rsem,
            device_id=at(me, z=sign * d), device_id_type=MESH,
        )
        wanted.append((jnp.logical_or(core == 0, goal >= 8), copy))
        when(wanted[-1][0], lambda copy=copy: copy.start())
    holds = jnp.logical_and(core == 1, jnp.logical_not(late))
    for goal in (2, 3, 4, 5, 6, 7):
        for c in (0, 1):
            copy = pltpu.make_async_remote_copy(
                q_buf.at[first + c], q_buf.at[first + c], fwd_ssem, q_rsem,
                device_id=at(me, z=goal - z + 16), device_id_type=MESH,
            )
            wanted.append((jnp.logical_and(holds, z >= 4 if goal < 4 else z < 4), copy))
            when(wanted[-1][0], lambda copy=copy: copy.start())

    arrived(t_recv, t_rsem)
    for k in range(4):
        x_buf[:, 128 * k : 128 * k + 128] = t_recv[:, k, :].astype(BF16)
    arrived(q_buf.at[pl.ds(0, 14)], q_rsem)
    part = nt(x_buf[...], q_buf[...].reshape(256, 512)) * (1.0 / 64)
    for k in range(2):
        s_send[:, k, :] = part[:, 128 * k : 128 * k + 128]
    place = (me["x_lo"] * 2 + core) * 8 + tensor
    for s, off in sorted(enumerate(PLANE), key=lambda p: -hops(difference(OPPOSITE, p[1]))):
        if off == OPPOSITE:
            pltpu.make_async_copy(s_send.at[s], s_recv.at[place], s_rsem).start()
            continue
        pltpu.make_async_remote_copy(
            s_send.at[s], s_recv.at[place], s_ssem, s_rsem, device_id=device[difference(OPPOSITE, off)], device_id_type=MESH
        ).start()

    arrived(part_send.at[pl.ds(0, 7)], part_ssem)
    arrived(t_recv.at[pl.ds(0, 31)], t_ssem)
    whole.wait_send()
    arrived(q_buf.at[pl.ds(0, 2)], far_ssem)
    for goes, copy in directs:
        when(goes, lambda copy=copy: copy.wait_send())
    for d in (3, -3, 2, -2, 1, -1):
        when(jnp.logical_or(jnp.logical_not(late), (z + d) // 8 == half), lambda d=d: near(d).wait_send())
    for condition, copy in wanted:
        when(condition, lambda copy=copy: copy.wait_send())
    when(half != core, lambda: sibling.wait_send())

    whole.wait_recv()
    tg_out[...] = tg_recv[...]

    arrived(s_recv, s_rsem)
    for w in range(4):
        scores_out[2 * w : 2 * w + 2, :] = jnp.sum(s_recv[8 * w : 8 * w + 8], axis=0)
    arrived(s_recv.at[pl.ds(0, 31)], s_ssem)


def finish(tg, part, tg_out, scores_out):
    tg_out[...] = tg[...].reshape(1, 4096)
    scores_out[...] = part[...].reshape(1, 1024)


def local(hidden_acts, out_grads, proj_in, proj_out, queries):
    dma = pltpu.SemaphoreType.DMA
    tg, scores = pl.pallas_call(
        kernel,
        name="influence",
        out_shape=(jax.ShapeDtypeStruct((32, 128), BF16), jax.ShapeDtypeStruct((8, 128), F32)),
        in_specs=[pl.BlockSpec(memory_space=pl.ANY)] * 5,
        out_specs=(pl.BlockSpec(memory_space=pltpu.VMEM),) * 2,
        scratch_shapes=[
            pltpu.VMEM((8, 128, 1792), BF16),
            pltpu.VMEM((8, 128, 512), BF16),
            pltpu.VMEM((64, 1792), BF16),
            pltpu.VMEM((64, 512), BF16),
            pltpu.VMEM((4, 64, 128), F32),
            pltpu.VMEM((64, 512), BF16),
            pltpu.VMEM((8, 128, 128), BF16),
            pltpu.VMEM((8, 128, 128), BF16),
            pltpu.VMEM((8, 4, 128), F32),
            pltpu.VMEM((32, 4, 128), F32),
            pltpu.VMEM((32, 128), BF16),
            pltpu.VMEM((32, 128), BF16),
            pltpu.VMEM((16, 16, 512), BF16),
            pltpu.VMEM((16, 512), BF16),
            pltpu.VMEM((32, 512), BF16),
            pltpu.VMEM((32, 2, 128), F32),
            pltpu.VMEM((32, 2, 128), F32),
            dma((2,)), dma((2,)), dma((3,)),
        ] + [dma] * 15 + [pltpu.SemaphoreType.REGULAR],
        compiler_params=pltpu.CompilerParams(
            collective_id=0, has_side_effects=True, vmem_limit_bytes=539 * 1024 * 1024 // 10
        ),
    )(hidden_acts, out_grads, proj_in.T, proj_out.T, queries)
    return pl.pallas_call(
        finish,
        name="finish",
        out_shape=(jax.ShapeDtypeStruct((1, 4096), BF16), jax.ShapeDtypeStruct((1, 1024), F32)),
        in_specs=[pl.BlockSpec(memory_space=pltpu.VMEM)] * 2,
        out_specs=(pl.BlockSpec(memory_space=pltpu.VMEM),) * 2,
        compiler_params=pltpu.CompilerParams(vmem_limit_bytes=1024 * 1024),
    )(tg, scores)


def solution(mesh):
    in_specs = (
        P("dp", None, "tensor"),
        P("dp", None, "tensor"),
        P("tensor", None),
        P("tensor", None),
        P("dp", None),
    )
    out_specs = (P(("dp", "tensor"), None), P(("dp", "tensor"), None))
    return jax.shard_map(local, mesh=mesh, in_specs=in_specs, out_specs=out_specs, check_vma=False)
```

```python
import functools

import jax
import jax.numpy as jnp
from jax import lax
from jax.experimental import pallas as pl
from jax.experimental.pallas import tpu as pltpu
from jax.sharding import PartitionSpec as P

MESH = pl.DeviceIdType.MESH
SIZES = dict(x_lo=2, z=16, core=2, y=4, x_hi=2)
F32, BF16 = jnp.float32, jnp.bfloat16


def hops(offset):
    y, x_hi, x_lo, _ = offset
    return min(y, 4 - y) + (1 if x_lo else 2 * x_hi)


PLANE = sorted(
    ((y, h, l, c) for y in range(4) for h in range(2) for l in range(2) for c in range(2)),
    key=lambda o: (-hops(o), o == (0, 0, 0, 0), o),
)
TENSOR = [o for o in PLANE if o[2:] == (0, 0)]
OPPOSITE = (2, 1, 0, 0)


def position():
    dp, tensor = lax.axis_index("dp"), lax.axis_index("tensor")
    return dict(
        x_lo=dp // 32, z=lax.rem(dp // 2, 16), core=lax.rem(dp, 2), y=tensor // 2, x_hi=lax.rem(tensor, 2)
    )


def at(place, **offsets):
    moved = {k: lax.rem(v + offsets.get(k, 0) + SIZES[k], SIZES[k]) for k, v in place.items()}
    return {
        "dp": moved["x_lo"] * 32 + moved["z"] * 2 + moved["core"],
        "tensor": moved["y"] * 2 + moved["x_hi"],
    }


def plane_map(place):
    dp = {(l, c): at(place, x_lo=l, core=c)["dp"] for l in range(2) for c in range(2)}
    tensor = {(y, h): at(place, y=y, x_hi=h)["tensor"] for y in range(4) for h in range(2)}
    return {o: {"dp": dp[o[2:]], "tensor": tensor[o[:2]]} for o in PLANE}


def difference(a, b):
    return tuple((p - q) % n for p, q, n in zip(a, b, (4, 2, 2, 2)))


def nt(a, b):
    return lax.dot_general(a, b, (((1,), (1,)), ((), ())), preferred_element_type=F32)


def arrived(buffer, semaphore):
    pltpu.make_async_copy(buffer, buffer, semaphore).wait()


def kernel(
    hidden, grads, w_in, w_out, queries, tg_out, scores_out,
    h_buf, g_buf, win_buf, wout_raw, wout_f32, wout_buf,
    part_send, part_recv,
    t_send, t_recv, tg_send, tg_recv, q_buf, mine, x_buf, s_send, s_recv,
    h_sem, g_sem, w_sem,
    part_ssem, part_rsem, t_ssem, t_rsem, tg_ssem, tg_rsem,
    q_ssem, q_rsem, far_ssem, far_rsem, sib_ssem, fwd_ssem, s_ssem, s_rsem, direct_ssem, late_ready,
):
    me = position()
    tensor, z, core = lax.axis_index("tensor"), me["z"], me["core"]
    device = plane_map(me)

    loads = [
        pltpu.make_async_copy(w_out, wout_raw, w_sem.at[0]),
        pltpu.make_async_copy(w_in, win_buf, w_sem.at[1]),
        pltpu.make_async_copy(
            queries.at[:, pl.ds(pl.multiple_of(tensor * 512, 512), 512)], mine, w_sem.at[2]
        ),
    ]
    for c in loads:
        c.start()
    reads = []
    for k in range(2):
        four = pl.ds(4 * k, 4)
        pair = (
            pltpu.make_async_copy(grads.at[four], g_buf.at[four], g_sem.at[k]),
            pltpu.make_async_copy(hidden.at[four], h_buf.at[four], h_sem.at[k]),
        )
        for c in pair:
            c.start()
        reads.append(pair)

    late = z >= 8
    barrier = pltpu.get_barrier_semaphore()

    def say(semaphore, device):
        pl.semaphore_signal(semaphore, inc=1, device_id=device, device_id_type=MESH)

    def when(condition, action):
        pl.when(condition)(action)

    def to_line(semaphore, d):
        for c in (0, 1):
            say(semaphore, at(dict(me, core=c), z=d))

    def to_second_half():
        for far in range(8, 16):
            window = jnp.logical_or(far - z <= 4, far - z >= 12)
            when(jnp.logical_or(core == 1, window), functools.partial(to_line, barrier, far - z))

    when(jnp.logical_not(late), to_second_half)
    for off in PLANE[:-1]:
        say(barrier, device[off])
    for d in (4, -4, 3, -3, 2, -2, 1, -1):
        when((z + d) // 8 == z // 8, functools.partial(to_line, barrier, d))
    when(z < 3, lambda: [when(z + d < 8, functools.partial(to_line, barrier, d)) for d in (7, 6, 5)] and None)
    place = lax.rem(z, 8)
    same = jnp.minimum(place, 4) + jnp.minimum(7 - place, 4)
    close = jnp.where(z < 12, 12 - z, z - 11)
    expected = 31 + 2 * same + jnp.where(late, close + 8, 2 * jnp.maximum(z - 4, 0))

    loads[0].wait()
    for j in range(4):
        lanes = slice(128 * j, 128 * j + 128)
        wout_f32[j] = wout_raw[:, lanes].astype(F32)
        wout_buf[0:32, lanes] = wout_f32[j, pl.ds(0, 32, stride=2), :].astype(BF16)
        wout_buf[32:64, lanes] = wout_f32[j, pl.ds(1, 32, stride=2), :].astype(BF16)
    loads[1].wait()

    for k in range(2):
        for c in reads[k]:
            c.wait()
        four = pl.ds(4 * k, 4)
        a = nt(wout_buf[...], g_buf[four].reshape(512, 512)).astype(BF16)
        b = nt(win_buf[...], h_buf[four].reshape(512, 1792)).astype(BF16)
        for j in range(4):
            part_send[4 * k + j, 0:64, :] = a[:, 128 * j : 128 * j + 128]
            part_send[4 * k + j, 64:128, :] = b[:, 128 * j : 128 * j + 128]

    pl.semaphore_wait(barrier, expected)

    half = z // 8
    slot = place * 2 + core
    loads[2].wait()

    def near(d, ssem=q_ssem, rsem=q_rsem):
        if isinstance(d, int) and abs(d) == 4:
            ssem, rsem = far_ssem, far_rsem
        return pltpu.make_async_remote_copy(
            mine, q_buf.at[slot], ssem, rsem, device_id=at(dict(me, core=half), z=d), device_id_type=MESH
        )

    relay = lax.rem(z + 4, 8)
    high, low = z >= 12, jnp.logical_and(late, z < 12)

    def straight(goal):
        return near(16 + goal - z, direct_ssem)

    def from_second_half():
        @pl.when(z >= 12)
        def _():
            near(16 + relay - z, far_ssem, far_rsem).start()
            for goal in range(4):
                when(relay != goal, lambda goal=goal: straight(goal).start())

        @pl.when(z < 12)
        def _():
            near(16 + relay - z, far_ssem, far_rsem).start()
            for goal in (0, 1, 2):
                straight(goal).start()
            for j in (1, 2, 3):
                straight(4 + lax.rem(relay + j, 4)).start()

        for d in (4, 3, 2, 1):
            when(jnp.logical_and(z - d < 8, z < 12), functools.partial(to_line, late_ready, -d))
            when(z + d >= 16, functools.partial(to_line, late_ready, d))

    when(late, from_second_half)

    def to_first_three():
        for d in (7, 6, 5):
            when(z - d >= 0, functools.partial(to_line, late_ready, -d))
            when(z - d >= 0, lambda d=d: near(-d, direct_ssem).start())

    distant = jnp.logical_and(z >= 5, z < 8)

    for k, off in enumerate(TENSOR):
        example = device[difference(off, OPPOSITE)]["tensor"]
        if k == 7:
            pltpu.make_async_copy(part_send.at[example], part_recv.at[k], part_rsem).start()
            continue
        pltpu.make_async_remote_copy(
            part_send.at[example], part_recv.at[k], part_ssem, part_rsem,
            device_id=device[off], device_id_type=MESH,
        ).start()

    for d in (-4, 4, -3, 3, -2, 2, -1, 1):
        when((z + d) // 8 == half, lambda d=d: near(d).start())
    when(distant, to_first_three)
    sibling = near(0, sib_ssem)
    own = pltpu.make_async_copy(mine, q_buf.at[slot], q_rsem)
    when(half == core, lambda: own.start())
    when(half != core, lambda: sibling.start())
    arrived(part_recv, part_rsem)
    total = part_recv[0].astype(F32)
    for k in range(1, 8):
        total += part_recv[k].astype(F32)
    total = total.astype(BF16)
    act = total[64:128]
    both = nt(total[0:64], jnp.concatenate([act, act], axis=0))
    lane = lax.broadcasted_iota(jnp.int32, (32, 128), 1)
    rows = jnp.where(lane < 64, both[0:32], both[32:64]).astype(BF16)
    tg_send[...] = rows
    wide = rows.astype(F32)
    for k in range(8):
        t_send[k] = wide[4 * k : 4 * k + 4]

    for s, off in enumerate(PLANE[:-1]):
        target = device[off]
        pltpu.make_async_remote_copy(
            t_send.at[target["tensor"]], t_recv.at[s], t_ssem, t_rsem, device_id=target, device_id_type=MESH
        ).start()
    pltpu.make_async_copy(t_send.at[tensor], t_recv.at[31], t_rsem).start()
    whole = pltpu.make_async_remote_copy(
        tg_send, tg_recv, tg_ssem, tg_rsem, device_id=device[OPPOSITE], device_id_type=MESH
    )
    whole.start()

    up = (lax.rem(z + 12, 16) // 8) == core
    sign = jnp.where(up, 1, -1)
    first = lax.rem(lax.rem(z - 4 * sign + 16, 16), 8) * 2
    holds = jnp.logical_and(core == 1, jnp.logical_not(late))
    early = jnp.logical_and(holds, z >= 4)

    def pass_on(block, target):
        return pltpu.make_async_remote_copy(
            q_buf.at[block], q_buf.at[block], fwd_ssem, q_rsem, device_id=target, device_id_type=MESH
        )

    @pl.when(early)
    def _():
        arrived(q_buf.at[pl.ds(0, 2)], far_rsem)
        for goal in (3,):
            for c in (0, 1):
                pass_on(first + c, at(me, z=goal - z + 16)).start()

    @pl.when(jnp.logical_not(late))
    def _():
        answers = jnp.where(z < 4, 4 - z, z - 3) + jnp.maximum(3 - z, 0)
        pl.semaphore_wait(late_ready, 2 * answers)
        for d in (4, 3, 2, 1):
            when(z - d < 0, lambda d=d: near(-d).start())
            when(z + d >= 8, lambda d=d: near(d).start())

    lower = jnp.logical_and(holds, z < 4)

    @pl.when(lower)
    def _():
        arrived(q_buf.at[pl.ds(0, 2)], far_rsem)
        for goal in (4, 5, 6, 7):
            for c in (0, 1):
                pass_on(first + c, at(me, z=goal - z + 16)).start()

    wanted = []
    for c, d in ((None, 4), (0, 3), (1, 3), (0, 2), (1, 2), (0, 1), (1, 1)):
        block = first + (jnp.where(up, 0, 1) if c is None else c)
        goal = lax.rem(z + sign * d + 16, 16)
        wanted.append((jnp.logical_or(goal >= 8, jnp.logical_and(core == 0, z >= 4)), pass_on(block, at(me, z=sign * d))))

    @pl.when(jnp.logical_not(holds))
    def _():
        arrived(q_buf.at[pl.ds(0, 2)], far_rsem)
        for condition, copy in wanted:
            when(condition, lambda copy=copy: copy.start())

    arrived(t_recv, t_rsem)
    for k in range(4):
        x_buf[:, 128 * k : 128 * k + 128] = t_recv[:, k, :].astype(BF16)
    arrived(q_buf.at[pl.ds(0, 14)], q_rsem)
    part = nt(x_buf[...], q_buf[...].reshape(256, 512)) * (1.0 / 64)
    for k in range(2):
        s_send[:, k, :] = part[:, 128 * k : 128 * k + 128]
    place = (me["x_lo"] * 2 + core) * 8 + tensor
    for s, off in sorted(enumerate(PLANE), key=lambda p: -hops(difference(OPPOSITE, p[1]))):
        if off == OPPOSITE:
            pltpu.make_async_copy(s_send.at[s], s_recv.at[place], s_rsem).start()
            continue
        pltpu.make_async_remote_copy(
            s_send.at[s], s_recv.at[place], s_ssem, s_rsem, device_id=device[difference(OPPOSITE, off)], device_id_type=MESH
        ).start()

    arrived(part_send.at[pl.ds(0, 7)], part_ssem)
    arrived(t_recv.at[pl.ds(0, 31)], t_ssem)
    whole.wait_send()
    arrived(q_buf.at[pl.ds(0, 2)], far_ssem)
    when(high, lambda: arrived(q_buf.at[pl.ds(0, 3)], direct_ssem))
    when(low, lambda: arrived(q_buf.at[pl.ds(0, 6)], direct_ssem))
    for d in (7, 6, 5):
        when(jnp.logical_and(distant, z - d >= 0), lambda d=d: near(-d, direct_ssem).wait_send())
    for d in (3, -3, 2, -2, 1, -1):
        when(jnp.logical_or(jnp.logical_not(late), (z + d) // 8 == half), lambda d=d: near(d).wait_send())
    when(early, lambda: arrived(q_buf.at[pl.ds(0, 2)], fwd_ssem))
    when(lower, lambda: arrived(q_buf.at[pl.ds(0, 8)], fwd_ssem))
    for condition, copy in wanted:
        when(jnp.logical_and(jnp.logical_not(holds), condition), lambda copy=copy: copy.wait_send())
    when(half != core, lambda: sibling.wait_send())

    whole.wait_recv()
    tg_out[...] = tg_recv[...]

    arrived(s_recv, s_rsem)
    for w in range(4):
        scores_out[2 * w : 2 * w + 2, :] = jnp.sum(s_recv[8 * w : 8 * w + 8], axis=0)
    arrived(s_recv.at[pl.ds(0, 31)], s_ssem)


def finish(tg, part, tg_out, scores_out):
    tg_out[...] = tg[...].reshape(1, 4096)
    scores_out[...] = part[...].reshape(1, 1024)


def local(hidden_acts, out_grads, proj_in, proj_out, queries):
    dma = pltpu.SemaphoreType.DMA
    tg, scores = pl.pallas_call(
        kernel,
        name="influence",
        out_shape=(jax.ShapeDtypeStruct((32, 128), BF16), jax.ShapeDtypeStruct((8, 128), F32)),
        in_specs=[pl.BlockSpec(memory_space=pl.ANY)] * 5,
        out_specs=(pl.BlockSpec(memory_space=pltpu.VMEM),) * 2,
        scratch_shapes=[
            pltpu.VMEM((8, 128, 1792), BF16),
            pltpu.VMEM((8, 128, 512), BF16),
            pltpu.VMEM((64, 1792), BF16),
            pltpu.VMEM((64, 512), BF16),
            pltpu.VMEM((4, 64, 128), F32),
            pltpu.VMEM((64, 512), BF16),
            pltpu.VMEM((8, 128, 128), BF16),
            pltpu.VMEM((8, 128, 128), BF16),
            pltpu.VMEM((8, 4, 128), F32),
            pltpu.VMEM((32, 4, 128), F32),
            pltpu.VMEM((32, 128), BF16),
            pltpu.VMEM((32, 128), BF16),
            pltpu.VMEM((16, 16, 512), BF16),
            pltpu.VMEM((16, 512), BF16),
            pltpu.VMEM((32, 512), BF16),
            pltpu.VMEM((32, 2, 128), F32),
            pltpu.VMEM((32, 2, 128), F32),
            dma((2,)), dma((2,)), dma((3,)),
        ] + [dma] * 15 + [pltpu.SemaphoreType.REGULAR],
        compiler_params=pltpu.CompilerParams(
            collective_id=0, has_side_effects=True, vmem_limit_bytes=539 * 1024 * 1024 // 10
        ),
    )(hidden_acts, out_grads, proj_in.T, proj_out.T, queries)
    return pl.pallas_call(
        finish,
        name="finish",
        out_shape=(jax.ShapeDtypeStruct((1, 4096), BF16), jax.ShapeDtypeStruct((1, 1024), F32)),
        in_specs=[pl.BlockSpec(memory_space=pltpu.VMEM)] * 2,
        out_specs=(pl.BlockSpec(memory_space=pltpu.VMEM),) * 2,
        compiler_params=pltpu.CompilerParams(vmem_limit_bytes=1024 * 1024),
    )(tg, scores)


def solution(mesh):
    in_specs = (
        P("dp", None, "tensor"),
        P("dp", None, "tensor"),
        P("tensor", None),
        P("tensor", None),
        P("dp", None),
    )
    out_specs = (P(("dp", "tensor"), None), P(("dp", "tensor"), None))
    return jax.shard_map(local, mesh=mesh, in_specs=in_specs, out_specs=out_specs, check_vma=False)
```

```python
import functools

import jax
import jax.numpy as jnp
from jax import lax
from jax.experimental import pallas as pl
from jax.experimental.pallas import tpu as pltpu
from jax.sharding import PartitionSpec as P

MESH = pl.DeviceIdType.MESH
SIZES = dict(x_lo=2, z=16, core=2, y=4, x_hi=2)
F32, BF16 = jnp.float32, jnp.bfloat16


def hops(offset):
    y, x_hi, x_lo, _ = offset
    return min(y, 4 - y) + (1 if x_lo else 2 * x_hi)


PLANE = sorted(
    ((y, h, l, c) for y in range(4) for h in range(2) for l in range(2) for c in range(2)),
    key=lambda o: (-hops(o), o == (0, 0, 0, 0), o),
)
TENSOR = [o for o in PLANE if o[2:] == (0, 0)]
OPPOSITE = (2, 1, 0, 0)


def position():
    dp, tensor = lax.axis_index("dp"), lax.axis_index("tensor")
    return dict(
        x_lo=dp // 32, z=lax.rem(dp // 2, 16), core=lax.rem(dp, 2), y=tensor // 2, x_hi=lax.rem(tensor, 2)
    )


def at(place, **offsets):
    moved = {k: lax.rem(v + offsets.get(k, 0) + SIZES[k], SIZES[k]) for k, v in place.items()}
    return {
        "dp": moved["x_lo"] * 32 + moved["z"] * 2 + moved["core"],
        "tensor": moved["y"] * 2 + moved["x_hi"],
    }


def plane_map(place):
    dp = {(l, c): at(place, x_lo=l, core=c)["dp"] for l in range(2) for c in range(2)}
    tensor = {(y, h): at(place, y=y, x_hi=h)["tensor"] for y in range(4) for h in range(2)}
    return {o: {"dp": dp[o[2:]], "tensor": tensor[o[:2]]} for o in PLANE}


def difference(a, b):
    return tuple((p - q) % n for p, q, n in zip(a, b, (4, 2, 2, 2)))


def nt(a, b):
    return lax.dot_general(a, b, (((1,), (1,)), ((), ())), preferred_element_type=F32)


def arrived(buffer, semaphore):
    pltpu.make_async_copy(buffer, buffer, semaphore).wait()


def kernel(
    hidden, grads, w_in, w_out, queries, tg_out, scores_out,
    h_buf, g_buf, win_buf, wout_raw, wout_f32, wout_buf,
    part_send, part_recv,
    t_send, t_recv, tg_send, tg_recv, q_buf, mine, x_buf, s_send, s_recv,
    h_sem, g_sem, w_sem,
    part_ssem, part_rsem, t_ssem, t_rsem, tg_ssem, tg_rsem,
    q_ssem, q_rsem, far_ssem, far_rsem, sib_ssem, fwd_ssem, s_ssem, s_rsem, direct_ssem, late_ready,
):
    me = position()
    tensor, z, core = lax.axis_index("tensor"), me["z"], me["core"]
    device = plane_map(me)

    loads = [
        pltpu.make_async_copy(w_out, wout_raw, w_sem.at[0]),
        pltpu.make_async_copy(w_in, win_buf, w_sem.at[1]),
        pltpu.make_async_copy(
            queries.at[:, pl.ds(pl.multiple_of(tensor * 512, 512), 512)], mine, w_sem.at[2]
        ),
    ]
    for c in loads:
        c.start()
    reads = []
    for k in range(2):
        four = pl.ds(4 * k, 4)
        pair = (
            pltpu.make_async_copy(grads.at[four], g_buf.at[four], g_sem.at[k]),
            pltpu.make_async_copy(hidden.at[four], h_buf.at[four], h_sem.at[k]),
        )
        for c in pair:
            c.start()
        reads.append(pair)

    late = z >= 8
    barrier = pltpu.get_barrier_semaphore()

    def say(semaphore, device):
        pl.semaphore_signal(semaphore, inc=1, device_id=device, device_id_type=MESH)

    def when(condition, action):
        pl.when(condition)(action)

    def to_line(semaphore, d):
        for c in (0, 1):
            say(semaphore, at(dict(me, core=c), z=d))

    def to_second_half():
        for far in range(8, 16):
            window = jnp.logical_or(far - z <= 4, far - z >= 12)
            when(jnp.logical_or(core == 1, window), functools.partial(to_line, barrier, far - z))

    when(jnp.logical_not(late), to_second_half)
    for d in (4, -4, 3, -3):
        when((z + d) // 8 == z // 8, functools.partial(to_line, barrier, d))
    for off in PLANE[:-1]:
        say(barrier, device[off])
    for d in (2, -2, 1, -1):
        when((z + d) // 8 == z // 8, functools.partial(to_line, barrier, d))
    when(z < 3, lambda: [when(z + d < 8, functools.partial(to_line, barrier, d)) for d in (7, 6, 5)] and None)
    place = lax.rem(z, 8)
    same = jnp.minimum(place, 4) + jnp.minimum(7 - place, 4)
    close = jnp.where(z < 12, 12 - z, z - 11)
    expected = 31 + 2 * same + jnp.where(late, close + 8, 2 * jnp.maximum(z - 4, 0))

    loads[0].wait()
    for j in range(4):
        lanes = slice(128 * j, 128 * j + 128)
        wout_f32[j] = wout_raw[:, lanes].astype(F32)
        wout_buf[0:32, lanes] = wout_f32[j, pl.ds(0, 32, stride=2), :].astype(BF16)
        wout_buf[32:64, lanes] = wout_f32[j, pl.ds(1, 32, stride=2), :].astype(BF16)
    loads[1].wait()

    for k in range(2):
        for c in reads[k]:
            c.wait()
        four = pl.ds(4 * k, 4)
        a = nt(wout_buf[...], g_buf[four].reshape(512, 512)).astype(BF16)
        b = nt(win_buf[...], h_buf[four].reshape(512, 1792)).astype(BF16)
        for j in range(4):
            part_send[4 * k + j, 0:64, :] = a[:, 128 * j : 128 * j + 128]
            part_send[4 * k + j, 64:128, :] = b[:, 128 * j : 128 * j + 128]

    pl.semaphore_wait(barrier, expected)

    half = z // 8
    slot = place * 2 + core
    loads[2].wait()

    def near(d, ssem=q_ssem, rsem=q_rsem):
        if isinstance(d, int) and abs(d) == 4:
            ssem, rsem = far_ssem, far_rsem
        return pltpu.make_async_remote_copy(
            mine, q_buf.at[slot], ssem, rsem, device_id=at(dict(me, core=half), z=d), device_id_type=MESH
        )

    relay = lax.rem(z + 4, 8)
    high, low = z >= 12, jnp.logical_and(late, z < 12)

    def straight(goal):
        return near(16 + goal - z, direct_ssem)

    def from_second_half():
        @pl.when(z >= 12)
        def _():
            near(16 + relay - z, far_ssem, far_rsem).start()
            for goal in range(4):
                when(relay != goal, lambda goal=goal: straight(goal).start())

        @pl.when(z < 12)
        def _():
            near(16 + relay - z, far_ssem, far_rsem).start()
            for goal in (0, 1, 2):
                straight(goal).start()
            for j in (1, 2, 3):
                straight(4 + lax.rem(relay + j, 4)).start()

        for d in (4, 3, 2, 1):
            when(jnp.logical_and(z - d < 8, z < 12), functools.partial(to_line, late_ready, -d))
            when(z + d >= 16, functools.partial(to_line, late_ready, d))

    when(late, from_second_half)

    def to_first_three():
        for d in (7, 6, 5):
            when(z - d >= 0, functools.partial(to_line, late_ready, -d))
            when(z - d >= 0, lambda d=d: near(-d, direct_ssem).start())

    distant = jnp.logical_and(z >= 5, z < 8)

    for k, off in enumerate(TENSOR):
        example = device[difference(off, OPPOSITE)]["tensor"]
        if k == 7:
            pltpu.make_async_copy(part_send.at[example], part_recv.at[k], part_rsem).start()
            continue
        pltpu.make_async_remote_copy(
            part_send.at[example], part_recv.at[k], part_ssem, part_rsem,
            device_id=device[off], device_id_type=MESH,
        ).start()

    for d in (-4, 4, -3, 3, -2, 2, -1, 1):
        when((z + d) // 8 == half, lambda d=d: near(d).start())
    when(distant, to_first_three)
    sibling = near(0, sib_ssem)
    own = pltpu.make_async_copy(mine, q_buf.at[slot], q_rsem)
    when(half == core, lambda: own.start())
    when(half != core, lambda: sibling.start())
    arrived(part_recv, part_rsem)
    total = part_recv[0].astype(F32)
    for k in range(1, 8):
        total += part_recv[k].astype(F32)
    total = total.astype(BF16)
    act = total[64:128]
    both = nt(total[0:64], jnp.concatenate([act, act], axis=0))
    lane = lax.broadcasted_iota(jnp.int32, (32, 128), 1)
    rows = jnp.where(lane < 64, both[0:32], both[32:64]).astype(BF16)
    tg_send[...] = rows
    wide = rows.astype(F32)
    for k in range(8):
        t_send[k] = wide[4 * k : 4 * k + 4]

    for s, off in enumerate(PLANE[:-1]):
        target = device[off]
        pltpu.make_async_remote_copy(
            t_send.at[target["tensor"]], t_recv.at[s], t_ssem, t_rsem, device_id=target, device_id_type=MESH
        ).start()
    pltpu.make_async_copy(t_send.at[tensor], t_recv.at[31], t_rsem).start()
    whole = pltpu.make_async_remote_copy(
        tg_send, tg_recv, tg_ssem, tg_rsem, device_id=device[OPPOSITE], device_id_type=MESH
    )
    whole.start()

    up = (lax.rem(z + 12, 16) // 8) == core
    sign = jnp.where(up, 1, -1)
    first = lax.rem(lax.rem(z - 4 * sign + 16, 16), 8) * 2
    holds = jnp.logical_and(core == 1, jnp.logical_not(late))
    early = jnp.logical_and(holds, z >= 4)

    both_cores = pl.ds(first, 2)

    def pass_on(block, target):
        return pltpu.make_async_remote_copy(
            q_buf.at[block], q_buf.at[block], fwd_ssem, q_rsem, device_id=target, device_id_type=MESH
        )

    @pl.when(early)
    def _():
        arrived(q_buf.at[pl.ds(0, 2)], far_rsem)
        pass_on(both_cores, at(me, z=3 - z + 16)).start()

    @pl.when(jnp.logical_not(late))
    def _():
        answers = jnp.where(z < 4, 4 - z, z - 3) + jnp.maximum(3 - z, 0)
        pl.semaphore_wait(late_ready, 2 * answers)
        for d in (4, 3, 2, 1):
            when(z - d < 0, lambda d=d: near(-d).start())
            when(z + d >= 8, lambda d=d: near(d).start())

    lower = jnp.logical_and(holds, z < 4)

    @pl.when(lower)
    def _():
        arrived(q_buf.at[pl.ds(0, 2)], far_rsem)
        for goal in (4, 5, 6, 7):
            pass_on(both_cores, at(me, z=goal - z + 16)).start()

    wanted = []
    for d in (4, 3, 2, 1):
        block = first + jnp.where(up, 0, 1) if d == 4 else both_cores
        goal = lax.rem(z + sign * d + 16, 16)
        wanted.append((jnp.logical_or(goal >= 8, jnp.logical_and(core == 0, z >= 4)), pass_on(block, at(me, z=sign * d))))

    @pl.when(jnp.logical_not(holds))
    def _():
        arrived(q_buf.at[pl.ds(0, 2)], far_rsem)
        for condition, copy in wanted:
            when(condition, lambda copy=copy: copy.start())

    arrived(t_recv, t_rsem)
    for k in range(4):
        x_buf[:, 128 * k : 128 * k + 128] = t_recv[:, k, :].astype(BF16)
    arrived(q_buf.at[pl.ds(0, 14)], q_rsem)
    part = nt(x_buf[...], q_buf[...].reshape(256, 512)) * (1.0 / 64)
    for k in range(2):
        s_send[:, k, :] = part[:, 128 * k : 128 * k + 128]
    place = (me["x_lo"] * 2 + core) * 8 + tensor
    for s, off in sorted(enumerate(PLANE), key=lambda p: -hops(difference(OPPOSITE, p[1]))):
        if off == OPPOSITE:
            pltpu.make_async_copy(s_send.at[s], s_recv.at[place], s_rsem).start()
            continue
        pltpu.make_async_remote_copy(
            s_send.at[s], s_recv.at[place], s_ssem, s_rsem, device_id=device[difference(OPPOSITE, off)], device_id_type=MESH
        ).start()

    arrived(part_send.at[pl.ds(0, 7)], part_ssem)
    arrived(t_recv.at[pl.ds(0, 31)], t_ssem)
    whole.wait_send()
    arrived(q_buf.at[pl.ds(0, 2)], far_ssem)
    when(high, lambda: arrived(q_buf.at[pl.ds(0, 3)], direct_ssem))
    when(low, lambda: arrived(q_buf.at[pl.ds(0, 6)], direct_ssem))
    for d in (7, 6, 5):
        when(jnp.logical_and(distant, z - d >= 0), lambda d=d: near(-d, direct_ssem).wait_send())
    for d in (3, -3, 2, -2, 1, -1):
        when(jnp.logical_or(jnp.logical_not(late), (z + d) // 8 == half), lambda d=d: near(d).wait_send())
    when(early, lambda: arrived(q_buf.at[pl.ds(0, 2)], fwd_ssem))
    when(lower, lambda: arrived(q_buf.at[pl.ds(0, 8)], fwd_ssem))
    for condition, copy in wanted:
        when(jnp.logical_and(jnp.logical_not(holds), condition), lambda copy=copy: copy.wait_send())
    when(half != core, lambda: sibling.wait_send())

    whole.wait_recv()
    tg_out[...] = tg_recv[...]

    arrived(s_recv, s_rsem)
    for w in range(4):
        scores_out[2 * w : 2 * w + 2, :] = jnp.sum(s_recv[8 * w : 8 * w + 8], axis=0)
    arrived(s_recv.at[pl.ds(0, 31)], s_ssem)


def finish(tg, part, tg_out, scores_out):
    tg_out[...] = tg[...].reshape(1, 4096)
    scores_out[...] = part[...].reshape(1, 1024)


def local(hidden_acts, out_grads, proj_in, proj_out, queries):
    dma = pltpu.SemaphoreType.DMA
    tg, scores = pl.pallas_call(
        kernel,
        name="influence",
        out_shape=(jax.ShapeDtypeStruct((32, 128), BF16), jax.ShapeDtypeStruct((8, 128), F32)),
        in_specs=[pl.BlockSpec(memory_space=pl.ANY)] * 5,
        out_specs=(pl.BlockSpec(memory_space=pltpu.VMEM),) * 2,
        scratch_shapes=[
            pltpu.VMEM((8, 128, 1792), BF16),
            pltpu.VMEM((8, 128, 512), BF16),
            pltpu.VMEM((64, 1792), BF16),
            pltpu.VMEM((64, 512), BF16),
            pltpu.VMEM((4, 64, 128), F32),
            pltpu.VMEM((64, 512), BF16),
            pltpu.VMEM((8, 128, 128), BF16),
            pltpu.VMEM((8, 128, 128), BF16),
            pltpu.VMEM((8, 4, 128), F32),
            pltpu.VMEM((32, 4, 128), F32),
            pltpu.VMEM((32, 128), BF16),
            pltpu.VMEM((32, 128), BF16),
            pltpu.VMEM((16, 16, 512), BF16),
            pltpu.VMEM((16, 512), BF16),
            pltpu.VMEM((32, 512), BF16),
            pltpu.VMEM((32, 2, 128), F32),
            pltpu.VMEM((32, 2, 128), F32),
            dma((2,)), dma((2,)), dma((3,)),
        ] + [dma] * 15 + [pltpu.SemaphoreType.REGULAR],
        compiler_params=pltpu.CompilerParams(
            collective_id=0, has_side_effects=True, vmem_limit_bytes=539 * 1024 * 1024 // 10
        ),
    )(hidden_acts, out_grads, proj_in.T, proj_out.T, queries)
    return pl.pallas_call(
        finish,
        name="finish",
        out_shape=(jax.ShapeDtypeStruct((1, 4096), BF16), jax.ShapeDtypeStruct((1, 1024), F32)),
        in_specs=[pl.BlockSpec(memory_space=pltpu.VMEM)] * 2,
        out_specs=(pl.BlockSpec(memory_space=pltpu.VMEM),) * 2,
        compiler_params=pltpu.CompilerParams(vmem_limit_bytes=1024 * 1024),
    )(tg, scores)


def solution(mesh):
    in_specs = (
        P("dp", None, "tensor"),
        P("dp", None, "tensor"),
        P("tensor", None),
        P("tensor", None),
        P("dp", None),
    )
    out_specs = (P(("dp", "tensor"), None), P(("dp", "tensor"), None))
    return jax.shard_map(local, mesh=mesh, in_specs=in_specs, out_specs=out_specs, check_vma=False)
```

```python
import functools

import jax
import jax.numpy as jnp
from jax import lax
from jax.experimental import pallas as pl
from jax.experimental.pallas import tpu as pltpu
from jax.sharding import PartitionSpec as P

MESH = pl.DeviceIdType.MESH
SIZES = dict(x_lo=2, z=16, core=2, y=4, x_hi=2)
F32, BF16 = jnp.float32, jnp.bfloat16


def hops(offset):
    y, x_hi, x_lo, _ = offset
    return min(y, 4 - y) + (1 if x_lo else 2 * x_hi)


PLANE = sorted(
    ((y, h, l, c) for y in range(4) for h in range(2) for l in range(2) for c in range(2)),
    key=lambda o: (-hops(o), o == (0, 0, 0, 0), o),
)
TENSOR = [o for o in PLANE if o[2:] == (0, 0)]
OPPOSITE = (2, 1, 0, 0)


def position():
    dp, tensor = lax.axis_index("dp"), lax.axis_index("tensor")
    return dict(
        x_lo=dp // 32, z=lax.rem(dp // 2, 16), core=lax.rem(dp, 2), y=tensor // 2, x_hi=lax.rem(tensor, 2)
    )


def at(place, **offsets):
    moved = {k: lax.rem(v + offsets.get(k, 0) + SIZES[k], SIZES[k]) for k, v in place.items()}
    return {
        "dp": moved["x_lo"] * 32 + moved["z"] * 2 + moved["core"],
        "tensor": moved["y"] * 2 + moved["x_hi"],
    }


def plane_map(place):
    dp = {(l, c): at(place, x_lo=l, core=c)["dp"] for l in range(2) for c in range(2)}
    tensor = {(y, h): at(place, y=y, x_hi=h)["tensor"] for y in range(4) for h in range(2)}
    return {o: {"dp": dp[o[2:]], "tensor": tensor[o[:2]]} for o in PLANE}


def difference(a, b):
    return tuple((p - q) % n for p, q, n in zip(a, b, (4, 2, 2, 2)))


def nt(a, b):
    return lax.dot_general(a, b, (((1,), (1,)), ((), ())), preferred_element_type=F32)


def arrived(buffer, semaphore):
    pltpu.make_async_copy(buffer, buffer, semaphore).wait()


def kernel(
    hidden, grads, w_in, w_out, queries, tg_out, scores_out,
    h_buf, g_buf, win_buf, wout_raw, wout_f32, wout_buf,
    part_send, part_recv,
    t_send, t_recv, tg_send, tg_recv, q_buf, mine, x_buf, s_send, s_recv,
    h_sem, g_sem, w_sem,
    part_ssem, part_rsem, t_ssem, t_rsem, tg_ssem, tg_rsem,
    q_ssem, q_rsem, far_ssem, far_rsem, sib_ssem, fwd_ssem, s_ssem, s_rsem, direct_ssem, late_ready,
):
    me = position()
    tensor, z, core = lax.axis_index("tensor"), me["z"], me["core"]
    device = plane_map(me)

    loads = [
        pltpu.make_async_copy(w_out, wout_raw, w_sem.at[0]),
        pltpu.make_async_copy(w_in, win_buf, w_sem.at[1]),
        pltpu.make_async_copy(
            queries.at[:, pl.ds(pl.multiple_of(tensor * 512, 512), 512)], mine, w_sem.at[2]
        ),
    ]
    for c in loads:
        c.start()
    reads = []
    for k in range(2):
        four = pl.ds(4 * k, 4)
        pair = (
            pltpu.make_async_copy(grads.at[four], g_buf.at[four], g_sem.at[k]),
            pltpu.make_async_copy(hidden.at[four], h_buf.at[four], h_sem.at[k]),
        )
        for c in pair:
            c.start()
        reads.append(pair)

    late = z >= 8
    barrier = pltpu.get_barrier_semaphore()

    def say(semaphore, device):
        pl.semaphore_signal(semaphore, inc=1, device_id=device, device_id_type=MESH)

    def when(condition, action):
        pl.when(condition)(action)

    def to_line(semaphore, d):
        for c in (0, 1):
            say(semaphore, at(dict(me, core=c), z=d))

    def to_second_half():
        for far in range(8, 16):
            window = jnp.logical_or(far - z <= 4, far - z >= 12)
            when(jnp.logical_or(core == 1, window), functools.partial(to_line, barrier, far - z))

    when(jnp.logical_not(late), to_second_half)
    for d in (4, -4, 3, -3):
        when((z + d) // 8 == z // 8, functools.partial(to_line, barrier, d))
    for off in PLANE[:-1]:
        say(barrier, device[off])
    for d in (2, -2, 1, -1):
        when((z + d) // 8 == z // 8, functools.partial(to_line, barrier, d))
    when(z < 3, lambda: [when(z + d < 8, functools.partial(to_line, barrier, d)) for d in (7, 6, 5)] and None)
    place = lax.rem(z, 8)
    same = jnp.minimum(place, 4) + jnp.minimum(7 - place, 4)
    close = jnp.where(z < 12, 12 - z, z - 11)
    expected = 31 + 2 * same + jnp.where(late, close + 8, 2 * jnp.maximum(z - 4, 0))

    loads[0].wait()
    for j in range(4):
        lanes = slice(128 * j, 128 * j + 128)
        wout_f32[j] = wout_raw[:, lanes].astype(F32)
        wout_buf[0:32, lanes] = wout_f32[j, pl.ds(0, 32, stride=2), :].astype(BF16)
        wout_buf[32:64, lanes] = wout_f32[j, pl.ds(1, 32, stride=2), :].astype(BF16)
    loads[1].wait()

    for k in range(2):
        for c in reads[k]:
            c.wait()
        four = pl.ds(4 * k, 4)
        a = nt(wout_buf[...], g_buf[four].reshape(512, 512)).astype(BF16)
        b = nt(win_buf[...], h_buf[four].reshape(512, 1792)).astype(BF16)
        for j in range(4):
            part_send[4 * k + j, 0:64, :] = a[:, 128 * j : 128 * j + 128]
            part_send[4 * k + j, 64:128, :] = b[:, 128 * j : 128 * j + 128]

    pl.semaphore_wait(barrier, expected)

    half = z // 8
    slot = place * 2 + core
    loads[2].wait()

    def near(d, ssem=q_ssem, rsem=q_rsem):
        if isinstance(d, int) and abs(d) == 4:
            ssem, rsem = far_ssem, far_rsem
        return pltpu.make_async_remote_copy(
            mine, q_buf.at[slot], ssem, rsem, device_id=at(dict(me, core=half), z=d), device_id_type=MESH
        )

    relay = lax.rem(z + 4, 8)
    high, low = z >= 12, jnp.logical_and(late, z < 12)

    def straight(goal):
        return near(16 + goal - z, direct_ssem)

    def from_second_half():
        @pl.when(z >= 12)
        def _():
            near(16 + relay - z, far_ssem, far_rsem).start()
            for goal in range(4):
                when(relay != goal, lambda goal=goal: straight(goal).start())

        @pl.when(z < 12)
        def _():
            near(16 + relay - z, far_ssem, far_rsem).start()
            for goal in (0, 1, 2):
                straight(goal).start()
            for j in (1, 2, 3):
                straight(4 + lax.rem(relay + j, 4)).start()

        for d in (4, 3, 2, 1):
            when(jnp.logical_and(z - d < 8, z < 12), functools.partial(to_line, late_ready, -d))
            when(z + d >= 16, functools.partial(to_line, late_ready, d))

    when(late, from_second_half)

    def to_first_three():
        for d in (7, 6, 5):
            when(z - d >= 0, functools.partial(to_line, late_ready, -d))
            when(z - d >= 0, lambda d=d: near(-d, direct_ssem).start())

    distant = jnp.logical_and(z >= 5, z < 8)

    for k, off in enumerate(TENSOR):
        example = device[difference(off, OPPOSITE)]["tensor"]
        if k == 7:
            pltpu.make_async_copy(part_send.at[example], part_recv.at[k], part_rsem).start()
            continue
        pltpu.make_async_remote_copy(
            part_send.at[example], part_recv.at[k], part_ssem, part_rsem,
            device_id=device[off], device_id_type=MESH,
        ).start()

    for d in (-4, 4, -3, 3, -2, 2, -1, 1):
        when((z + d) // 8 == half, lambda d=d: near(d).start())
    when(distant, to_first_three)
    sibling = near(0, sib_ssem)
    own = pltpu.make_async_copy(mine, q_buf.at[slot], q_rsem)
    when(half == core, lambda: own.start())
    when(half != core, lambda: sibling.start())
    arrived(part_recv, part_rsem)
    total = part_recv[0].astype(F32)
    for k in range(1, 8):
        total += part_recv[k].astype(F32)
    total = total.astype(BF16)
    act = total[64:128]
    both = nt(total[0:64], jnp.concatenate([act, act], axis=0))
    lane = lax.broadcasted_iota(jnp.int32, (32, 128), 1)
    rows = jnp.where(lane < 64, both[0:32], both[32:64]).astype(BF16)
    tg_send[...] = rows
    wide = rows.astype(F32)
    for k in range(8):
        t_send[k] = wide[4 * k : 4 * k + 4]

    for s, off in enumerate(PLANE[:-1]):
        target = device[off]
        pltpu.make_async_remote_copy(
            t_send.at[target["tensor"]], t_recv.at[s], t_ssem, t_rsem, device_id=target, device_id_type=MESH
        ).start()
    pltpu.make_async_copy(t_send.at[tensor], t_recv.at[31], t_rsem).start()
    whole = pltpu.make_async_remote_copy(
        tg_send, tg_recv, tg_ssem, tg_rsem, device_id=device[OPPOSITE], device_id_type=MESH
    )
    whole.start()

    up = (lax.rem(z + 12, 16) // 8) == core
    sign = jnp.where(up, 1, -1)
    first = lax.rem(lax.rem(z - 4 * sign + 16, 16), 8) * 2
    holds = jnp.logical_and(core == 1, jnp.logical_not(late))
    early = jnp.logical_and(holds, z >= 4)

    both_cores = pl.ds(first, 2)

    def pass_on(block, target):
        return pltpu.make_async_remote_copy(
            q_buf.at[block], q_buf.at[block], fwd_ssem, q_rsem, device_id=target, device_id_type=MESH
        )

    @pl.when(early)
    def _():
        arrived(q_buf.at[pl.ds(0, 2)], far_rsem)
        pass_on(both_cores, at(me, z=3 - z + 16)).start()

    @pl.when(jnp.logical_not(late))
    def _():
        answers = jnp.where(z < 4, 4 - z, z - 3) + jnp.maximum(3 - z, 0)
        pl.semaphore_wait(late_ready, 2 * answers)
        for d in (4, 3, 2, 1):
            when(z - d < 0, lambda d=d: near(-d).start())
            when(z + d >= 8, lambda d=d: near(d).start())

    lower = jnp.logical_and(holds, z < 4)

    @pl.when(lower)
    def _():
        arrived(q_buf.at[pl.ds(0, 2)], far_rsem)
        for goal in (4, 5, 6, 7):
            pass_on(both_cores, at(me, z=goal - z + 16)).start()

    wanted = []
    for d in (4, 3, 2, 1):
        block = first + jnp.where(up, 0, 1) if d == 4 else both_cores
        goal = lax.rem(z + sign * d + 16, 16)
        wanted.append((jnp.logical_or(goal >= 8, jnp.logical_and(core == 0, z >= 4)), pass_on(block, at(me, z=sign * d))))

    @pl.when(jnp.logical_not(holds))
    def _():
        arrived(q_buf.at[pl.ds(0, 2)], far_rsem)
        for condition, copy in wanted:
            when(condition, lambda copy=copy: copy.start())

    arrived(t_recv, t_rsem)
    for k in range(4):
        x_buf[:, 128 * k : 128 * k + 128] = t_recv[:, k, :].astype(BF16)
    arrived(q_buf.at[pl.ds(0, 14)], q_rsem)
    part = nt(x_buf[...], q_buf[...].reshape(256, 512))
    for k in range(2):
        s_send[:, k, :] = part[:, 128 * k : 128 * k + 128]
    place = (me["x_lo"] * 2 + core) * 8 + tensor
    for s, off in sorted(enumerate(PLANE), key=lambda p: -hops(difference(OPPOSITE, p[1]))):
        if off == OPPOSITE:
            pltpu.make_async_copy(s_send.at[s], s_recv.at[place], s_rsem).start()
            continue
        pltpu.make_async_remote_copy(
            s_send.at[s], s_recv.at[place], s_ssem, s_rsem, device_id=device[difference(OPPOSITE, off)], device_id_type=MESH
        ).start()

    arrived(part_send.at[pl.ds(0, 7)], part_ssem)
    arrived(t_recv.at[pl.ds(0, 31)], t_ssem)
    whole.wait_send()
    arrived(q_buf.at[pl.ds(0, 2)], far_ssem)
    when(high, lambda: arrived(q_buf.at[pl.ds(0, 3)], direct_ssem))
    when(low, lambda: arrived(q_buf.at[pl.ds(0, 6)], direct_ssem))
    for d in (7, 6, 5):
        when(jnp.logical_and(distant, z - d >= 0), lambda d=d: near(-d, direct_ssem).wait_send())
    for d in (3, -3, 2, -2, 1, -1):
        when(jnp.logical_or(jnp.logical_not(late), (z + d) // 8 == half), lambda d=d: near(d).wait_send())
    when(early, lambda: arrived(q_buf.at[pl.ds(0, 2)], fwd_ssem))
    when(lower, lambda: arrived(q_buf.at[pl.ds(0, 8)], fwd_ssem))
    for condition, copy in wanted:
        when(jnp.logical_and(jnp.logical_not(holds), condition), lambda copy=copy: copy.wait_send())
    when(half != core, lambda: sibling.wait_send())

    whole.wait_recv()
    tg_out[...] = tg_recv[...]

    arrived(s_recv, s_rsem)
    for w in range(4):
        scores_out[2 * w : 2 * w + 2, :] = jnp.sum(s_recv[8 * w : 8 * w + 8], axis=0) * (1.0 / 64)
    arrived(s_recv.at[pl.ds(0, 31)], s_ssem)


def finish(tg, part, tg_out, scores_out):
    tg_out[...] = tg[...].reshape(1, 4096)
    scores_out[...] = part[...].reshape(1, 1024)


def local(hidden_acts, out_grads, proj_in, proj_out, queries):
    dma = pltpu.SemaphoreType.DMA
    tg, scores = pl.pallas_call(
        kernel,
        name="influence",
        out_shape=(jax.ShapeDtypeStruct((32, 128), BF16), jax.ShapeDtypeStruct((8, 128), F32)),
        in_specs=[pl.BlockSpec(memory_space=pl.ANY)] * 5,
        out_specs=(pl.BlockSpec(memory_space=pltpu.VMEM),) * 2,
        scratch_shapes=[
            pltpu.VMEM((8, 128, 1792), BF16),
            pltpu.VMEM((8, 128, 512), BF16),
            pltpu.VMEM((64, 1792), BF16),
            pltpu.VMEM((64, 512), BF16),
            pltpu.VMEM((4, 64, 128), F32),
            pltpu.VMEM((64, 512), BF16),
            pltpu.VMEM((8, 128, 128), BF16),
            pltpu.VMEM((8, 128, 128), BF16),
            pltpu.VMEM((8, 4, 128), F32),
            pltpu.VMEM((32, 4, 128), F32),
            pltpu.VMEM((32, 128), BF16),
            pltpu.VMEM((32, 128), BF16),
            pltpu.VMEM((16, 16, 512), BF16),
            pltpu.VMEM((16, 512), BF16),
            pltpu.VMEM((32, 512), BF16),
            pltpu.VMEM((32, 2, 128), F32),
            pltpu.VMEM((32, 2, 128), F32),
            dma((2,)), dma((2,)), dma((3,)),
        ] + [dma] * 15 + [pltpu.SemaphoreType.REGULAR],
        compiler_params=pltpu.CompilerParams(
            collective_id=0, has_side_effects=True, vmem_limit_bytes=539 * 1024 * 1024 // 10
        ),
    )(hidden_acts, out_grads, proj_in.T, proj_out.T, queries)
    return pl.pallas_call(
        finish,
        name="finish",
        out_shape=(jax.ShapeDtypeStruct((1, 4096), BF16), jax.ShapeDtypeStruct((1, 1024), F32)),
        in_specs=[pl.BlockSpec(memory_space=pltpu.VMEM)] * 2,
        out_specs=(pl.BlockSpec(memory_space=pltpu.VMEM),) * 2,
        compiler_params=pltpu.CompilerParams(vmem_limit_bytes=1024 * 1024),
    )(tg, scores)


def solution(mesh):
    in_specs = (
        P("dp", None, "tensor"),
        P("dp", None, "tensor"),
        P("tensor", None),
        P("tensor", None),
        P("dp", None),
    )
    out_specs = (P(("dp", "tensor"), None), P(("dp", "tensor"), None))
    return jax.shard_map(local, mesh=mesh, in_specs=in_specs, out_specs=out_specs, check_vma=False)
```

```python
import functools

import jax
import jax.numpy as jnp
from jax import lax
from jax.experimental import pallas as pl
from jax.experimental.pallas import tpu as pltpu
from jax.sharding import PartitionSpec as P

MESH = pl.DeviceIdType.MESH
SIZES = dict(x_lo=2, z=16, core=2, y=4, x_hi=2)
F32, BF16 = jnp.float32, jnp.bfloat16


def hops(offset):
    y, x_hi, x_lo, _ = offset
    return min(y, 4 - y) + (1 if x_lo else 2 * x_hi)


PLANE = sorted(
    ((y, h, l, c) for y in range(4) for h in range(2) for l in range(2) for c in range(2)),
    key=lambda o: (-hops(o), o == (0, 0, 0, 0), o),
)
TENSOR = [o for o in PLANE if o[2:] == (0, 0)]
OPPOSITE = (2, 1, 0, 0)


def position():
    dp, tensor = lax.axis_index("dp"), lax.axis_index("tensor")
    return dict(
        x_lo=dp // 32, z=lax.rem(dp // 2, 16), core=lax.rem(dp, 2), y=tensor // 2, x_hi=lax.rem(tensor, 2)
    )


def at(place, **offsets):
    moved = {k: lax.rem(v + offsets.get(k, 0) + SIZES[k], SIZES[k]) for k, v in place.items()}
    return {
        "dp": moved["x_lo"] * 32 + moved["z"] * 2 + moved["core"],
        "tensor": moved["y"] * 2 + moved["x_hi"],
    }


def plane_map(place):
    dp = {(l, c): at(place, x_lo=l, core=c)["dp"] for l in range(2) for c in range(2)}
    tensor = {(y, h): at(place, y=y, x_hi=h)["tensor"] for y in range(4) for h in range(2)}
    return {o: {"dp": dp[o[2:]], "tensor": tensor[o[:2]]} for o in PLANE}


def difference(a, b):
    return tuple((p - q) % n for p, q, n in zip(a, b, (4, 2, 2, 2)))


def nt(a, b):
    return lax.dot_general(a, b, (((1,), (1,)), ((), ())), preferred_element_type=F32)


def arrived(buffer, semaphore):
    pltpu.make_async_copy(buffer, buffer, semaphore).wait()


def kernel(
    hidden, grads, w_in, w_out, queries, tg_out, scores_out,
    h_buf, g_buf, win_buf, wout_raw, wout_f32, wout_buf,
    part_send, part_recv,
    t_send, t_recv, tg_send, tg_recv, q_buf, mine, x_buf, s_send, s_recv,
    h_sem, g_sem, w_sem,
    part_ssem, part_rsem, t_ssem, t_rsem, tg_ssem, tg_rsem,
    q_ssem, q_rsem, far_ssem, far_rsem, sib_ssem, fwd_ssem, s_ssem, s_rsem, direct_ssem, late_ready,
):
    me = position()
    tensor, z, core = lax.axis_index("tensor"), me["z"], me["core"]
    device = plane_map(me)

    loads = [
        pltpu.make_async_copy(w_out, wout_raw, w_sem.at[0]),
        pltpu.make_async_copy(w_in, win_buf, w_sem.at[1]),
        pltpu.make_async_copy(
            queries.at[:, pl.ds(pl.multiple_of(tensor * 512, 512), 512)], mine, w_sem.at[2]
        ),
    ]
    for c in loads:
        c.start()
    reads = []
    for k in range(2):
        four = pl.ds(4 * k, 4)
        pair = (
            pltpu.make_async_copy(grads.at[four], g_buf.at[four], g_sem.at[k]),
            pltpu.make_async_copy(hidden.at[four], h_buf.at[four], h_sem.at[k]),
        )
        for c in pair:
            c.start()
        reads.append(pair)

    late = z >= 8
    barrier = pltpu.get_barrier_semaphore()

    def say(semaphore, device):
        pl.semaphore_signal(semaphore, inc=1, device_id=device, device_id_type=MESH)

    def when(condition, action):
        pl.when(condition)(action)

    def to_line(semaphore, d):
        for c in (0, 1):
            say(semaphore, at(dict(me, core=c), z=d))

    def to_second_half():
        for far in range(8, 16):
            window = jnp.logical_or(far - z <= 4, far - z >= 12)
            when(jnp.logical_or(core == 1, window), functools.partial(to_line, barrier, far - z))

    when(jnp.logical_not(late), to_second_half)
    for d in (4, -4, 3, -3):
        when((z + d) // 8 == z // 8, functools.partial(to_line, barrier, d))
    for off in PLANE[:-1]:
        say(barrier, device[off])
    for d in (2, -2, 1, -1):
        when((z + d) // 8 == z // 8, functools.partial(to_line, barrier, d))
    when(z < 3, lambda: [when(z + d < 8, functools.partial(to_line, barrier, d)) for d in (7, 6, 5)] and None)
    place = lax.rem(z, 8)
    same = jnp.minimum(place, 4) + jnp.minimum(7 - place, 4)
    close = jnp.where(z < 12, 12 - z, z - 11)
    expected = 31 + 2 * same + jnp.where(late, close + 8, 2 * jnp.maximum(z - 4, 0))

    loads[0].wait()
    for j in range(4):
        lanes = slice(128 * j, 128 * j + 128)
        wout_f32[j] = wout_raw[:, lanes].astype(F32)
        wout_buf[0:32, lanes] = wout_f32[j, pl.ds(0, 32, stride=2), :].astype(BF16)
        wout_buf[32:64, lanes] = wout_f32[j, pl.ds(1, 32, stride=2), :].astype(BF16)
    loads[1].wait()

    for k in range(2):
        for c in reads[k]:
            c.wait()
        four = pl.ds(4 * k, 4)
        a = nt(wout_buf[...], g_buf[four].reshape(512, 512)).astype(BF16)
        b = nt(win_buf[...], h_buf[four].reshape(512, 1792)).astype(BF16)
        for j in range(4):
            part_send[4 * k + j, 0:64, :] = a[:, 128 * j : 128 * j + 128]
            part_send[4 * k + j, 64:128, :] = b[:, 128 * j : 128 * j + 128]

    pl.semaphore_wait(barrier, expected)

    half = z // 8
    slot = place * 2 + core
    loads[2].wait()

    def near(d, ssem=q_ssem, rsem=q_rsem):
        if isinstance(d, int) and abs(d) == 4:
            ssem, rsem = far_ssem, far_rsem
        return pltpu.make_async_remote_copy(
            mine, q_buf.at[slot], ssem, rsem, device_id=at(dict(me, core=half), z=d), device_id_type=MESH
        )

    relay = lax.rem(z + 4, 8)
    high, low = z >= 12, jnp.logical_and(late, z < 12)

    def straight(goal):
        return near(16 + goal - z, direct_ssem)

    def from_second_half():
        @pl.when(z >= 12)
        def _():
            near(16 + relay - z, far_ssem, far_rsem).start()
            for goal in range(4):
                when(relay != goal, lambda goal=goal: straight(goal).start())

        @pl.when(z < 12)
        def _():
            near(16 + relay - z, far_ssem, far_rsem).start()
            for goal in (0, 1, 2):
                straight(goal).start()
            for j in (1, 2, 3):
                straight(4 + lax.rem(relay + j, 4)).start()

        for d in (4, 3, 2, 1):
            when(jnp.logical_and(z - d < 8, z < 12), functools.partial(to_line, late_ready, -d))
            when(z + d >= 16, functools.partial(to_line, late_ready, d))

    when(late, from_second_half)

    def to_first_three():
        for d in (7, 6, 5):
            when(z - d >= 0, functools.partial(to_line, late_ready, -d))
            when(z - d >= 0, lambda d=d: near(-d, direct_ssem).start())

    distant = jnp.logical_and(z >= 5, z < 8)

    for d in (-4, 4, -3, 3, -2, 2, -1, 1):
        when((z + d) // 8 == half, lambda d=d: near(d).start())
    for k, off in enumerate(TENSOR):
        example = device[difference(off, OPPOSITE)]["tensor"]
        if k == 7:
            pltpu.make_async_copy(part_send.at[example], part_recv.at[k], part_rsem).start()
            continue
        pltpu.make_async_remote_copy(
            part_send.at[example], part_recv.at[k], part_ssem, part_rsem,
            device_id=device[off], device_id_type=MESH,
        ).start()

    when(distant, to_first_three)
    sibling = near(0, sib_ssem)
    own = pltpu.make_async_copy(mine, q_buf.at[slot], q_rsem)
    when(half == core, lambda: own.start())
    when(half != core, lambda: sibling.start())
    arrived(part_recv, part_rsem)
    total = part_recv[0].astype(F32)
    for k in range(1, 8):
        total += part_recv[k].astype(F32)
    total = total.astype(BF16)
    act = total[64:128]
    both = nt(total[0:64], jnp.concatenate([act, act], axis=0))
    lane = lax.broadcasted_iota(jnp.int32, (32, 128), 1)
    rows = jnp.where(lane < 64, both[0:32], both[32:64]).astype(BF16)
    tg_send[...] = rows
    wide = rows.astype(F32)
    for k in range(8):
        t_send[k] = wide[4 * k : 4 * k + 4]

    for s, off in enumerate(PLANE[:-1]):
        target = device[off]
        pltpu.make_async_remote_copy(
            t_send.at[target["tensor"]], t_recv.at[s], t_ssem, t_rsem, device_id=target, device_id_type=MESH
        ).start()
    pltpu.make_async_copy(t_send.at[tensor], t_recv.at[31], t_rsem).start()
    whole = pltpu.make_async_remote_copy(
        tg_send, tg_recv, tg_ssem, tg_rsem, device_id=device[OPPOSITE], device_id_type=MESH
    )
    whole.start()

    up = (lax.rem(z + 12, 16) // 8) == core
    sign = jnp.where(up, 1, -1)
    first = lax.rem(lax.rem(z - 4 * sign + 16, 16), 8) * 2
    holds = jnp.logical_and(core == 1, jnp.logical_not(late))
    early = jnp.logical_and(holds, z >= 4)

    both_cores = pl.ds(first, 2)

    def pass_on(block, target):
        return pltpu.make_async_remote_copy(
            q_buf.at[block], q_buf.at[block], fwd_ssem, q_rsem, device_id=target, device_id_type=MESH
        )

    @pl.when(early)
    def _():
        arrived(q_buf.at[pl.ds(0, 2)], far_rsem)
        pass_on(both_cores, at(me, z=3 - z + 16)).start()

    @pl.when(jnp.logical_not(late))
    def _():
        answers = jnp.where(z < 4, 4 - z, z - 3) + jnp.maximum(3 - z, 0)
        pl.semaphore_wait(late_ready, 2 * answers)
        for d in (4, 3, 2, 1):
            when(z - d < 0, lambda d=d: near(-d).start())
            when(z + d >= 8, lambda d=d: near(d).start())

    lower = jnp.logical_and(holds, z < 4)

    @pl.when(lower)
    def _():
        arrived(q_buf.at[pl.ds(0, 2)], far_rsem)
        for goal in (4, 5, 6, 7):
            pass_on(both_cores, at(me, z=goal - z + 16)).start()

    wanted = []
    for d in (4, 3, 2, 1):
        block = first + jnp.where(up, 0, 1) if d == 4 else both_cores
        goal = lax.rem(z + sign * d + 16, 16)
        wanted.append((jnp.logical_or(goal >= 8, jnp.logical_and(core == 0, z >= 4)), pass_on(block, at(me, z=sign * d))))

    @pl.when(jnp.logical_not(holds))
    def _():
        arrived(q_buf.at[pl.ds(0, 2)], far_rsem)
        for condition, copy in wanted:
            when(condition, lambda copy=copy: copy.start())

    arrived(t_recv, t_rsem)
    for k in range(4):
        x_buf[:, 128 * k : 128 * k + 128] = t_recv[:, k, :].astype(BF16)
    arrived(q_buf.at[pl.ds(0, 14)], q_rsem)
    part = nt(x_buf[...], q_buf[...].reshape(256, 512))
    for k in range(2):
        s_send[:, k, :] = part[:, 128 * k : 128 * k + 128]
    place = (me["x_lo"] * 2 + core) * 8 + tensor
    for s, off in sorted(enumerate(PLANE), key=lambda p: -hops(difference(OPPOSITE, p[1]))):
        if off == OPPOSITE:
            pltpu.make_async_copy(s_send.at[s], s_recv.at[place], s_rsem).start()
            continue
        pltpu.make_async_remote_copy(
            s_send.at[s], s_recv.at[place], s_ssem, s_rsem, device_id=device[difference(OPPOSITE, off)], device_id_type=MESH
        ).start()

    arrived(part_send.at[pl.ds(0, 7)], part_ssem)
    arrived(t_recv.at[pl.ds(0, 31)], t_ssem)
    whole.wait_send()
    arrived(q_buf.at[pl.ds(0, 2)], far_ssem)
    when(high, lambda: arrived(q_buf.at[pl.ds(0, 3)], direct_ssem))
    when(low, lambda: arrived(q_buf.at[pl.ds(0, 6)], direct_ssem))
    for d in (7, 6, 5):
        when(jnp.logical_and(distant, z - d >= 0), lambda d=d: near(-d, direct_ssem).wait_send())
    for d in (3, -3, 2, -2, 1, -1):
        when(jnp.logical_or(jnp.logical_not(late), (z + d) // 8 == half), lambda d=d: near(d).wait_send())
    when(early, lambda: arrived(q_buf.at[pl.ds(0, 2)], fwd_ssem))
    when(lower, lambda: arrived(q_buf.at[pl.ds(0, 8)], fwd_ssem))
    for condition, copy in wanted:
        when(jnp.logical_and(jnp.logical_not(holds), condition), lambda copy=copy: copy.wait_send())
    when(half != core, lambda: sibling.wait_send())

    whole.wait_recv()
    tg_out[...] = tg_recv[...]

    arrived(s_recv, s_rsem)
    for w in range(4):
        scores_out[2 * w : 2 * w + 2, :] = jnp.sum(s_recv[8 * w : 8 * w + 8], axis=0) * (1.0 / 64)
    arrived(s_recv.at[pl.ds(0, 31)], s_ssem)


def finish(tg, part, tg_out, scores_out):
    tg_out[...] = tg[...].reshape(1, 4096)
    scores_out[...] = part[...].reshape(1, 1024)


def local(hidden_acts, out_grads, proj_in, proj_out, queries):
    dma = pltpu.SemaphoreType.DMA
    tg, scores = pl.pallas_call(
        kernel,
        name="influence",
        out_shape=(jax.ShapeDtypeStruct((32, 128), BF16), jax.ShapeDtypeStruct((8, 128), F32)),
        in_specs=[pl.BlockSpec(memory_space=pl.ANY)] * 5,
        out_specs=(pl.BlockSpec(memory_space=pltpu.VMEM),) * 2,
        scratch_shapes=[
            pltpu.VMEM((8, 128, 1792), BF16),
            pltpu.VMEM((8, 128, 512), BF16),
            pltpu.VMEM((64, 1792), BF16),
            pltpu.VMEM((64, 512), BF16),
            pltpu.VMEM((4, 64, 128), F32),
            pltpu.VMEM((64, 512), BF16),
            pltpu.VMEM((8, 128, 128), BF16),
            pltpu.VMEM((8, 128, 128), BF16),
            pltpu.VMEM((8, 4, 128), F32),
            pltpu.VMEM((32, 4, 128), F32),
            pltpu.VMEM((32, 128), BF16),
            pltpu.VMEM((32, 128), BF16),
            pltpu.VMEM((16, 16, 512), BF16),
            pltpu.VMEM((16, 512), BF16),
            pltpu.VMEM((32, 512), BF16),
            pltpu.VMEM((32, 2, 128), F32),
            pltpu.VMEM((32, 2, 128), F32),
            dma((2,)), dma((2,)), dma((3,)),
        ] + [dma] * 15 + [pltpu.SemaphoreType.REGULAR],
        compiler_params=pltpu.CompilerParams(
            collective_id=0, has_side_effects=True, vmem_limit_bytes=539 * 1024 * 1024 // 10
        ),
    )(hidden_acts, out_grads, proj_in.T, proj_out.T, queries)
    return pl.pallas_call(
        finish,
        name="finish",
        out_shape=(jax.ShapeDtypeStruct((1, 4096), BF16), jax.ShapeDtypeStruct((1, 1024), F32)),
        in_specs=[pl.BlockSpec(memory_space=pltpu.VMEM)] * 2,
        out_specs=(pl.BlockSpec(memory_space=pltpu.VMEM),) * 2,
        compiler_params=pltpu.CompilerParams(vmem_limit_bytes=1024 * 1024),
    )(tg, scores)


def solution(mesh):
    in_specs = (
        P("dp", None, "tensor"),
        P("dp", None, "tensor"),
        P("tensor", None),
        P("tensor", None),
        P("dp", None),
    )
    out_specs = (P(("dp", "tensor"), None), P(("dp", "tensor"), None))
    return jax.shard_map(local, mesh=mesh, in_specs=in_specs, out_specs=out_specs, check_vma=False)
```
